256 devices in a mesh: row: 64 (over y, x_hi, z), ch: 4 (over x_lo, core).
Axes of the slice: x: 4 (x_hi: 2, x_lo: 2; x = x_hi * 2 + x_lo), y: 4, z: 8, core: 2. Of those that a mesh axis runs over, the one named last changes fastest.
Arguments:
- pair_field: bfloat16 [128, 512, 512], P('ch', 'row'), may hold values from -25 to 25
- input_gain: float32 [128], replicated, may hold values from 0.5 to 1.5
- input_bias: float32 [128], replicated, may hold values from -1.2 to 1.2
- left_weight: bfloat16 [128, 128], P(None, 'ch'), may hold values from -0.5 to 0.5
- left_gate: bfloat16 [128, 128], P(None, 'ch'), may hold values from -0.5 to 0.5
- right_weight: bfloat16 [128, 128], P(None, 'ch'), may hold values from -0.5 to 0.5
- right_gate: bfloat16 [128, 128], P(None, 'ch'), may hold values from -0.5 to 0.5
- gate_weight: bfloat16 [128, 128], P(None, 'ch'), may hold values from -0.5 to 0.5
- output_gain: float32 [128], replicated, may hold values from 0.5 to 1.5
- output_bias: float32 [128], replicated, may hold values from -1.2 to 1.2
- final_weight: bfloat16 [128, 128], P(None, 'ch'), may hold values from -0.5 to 0.5
Outputs:
- transposed: bfloat16 [128, 512, 512], P('ch', 'row')
The draws below stay inside these ranges and needn't reach their ends.
All inputs are finite; a program needn't handle non-finite values.
Results may differ from the reference program's by a relative error of at most 0.012.
Values may be sent and summed in bfloat16 or wider, within the bound.
No kernel may reach another device: no remote copies, remote signals or barrier semaphores. Data moves between devices by JAX's collectives and lax.ppermute only.
A program may use at most 64 MiB of HBM per device.

```python
import math
import jax
import jax.numpy as jnp
from jax import lax

C = 128
CH = 128
N = 512


def draw_pair_field(key, part):
    key = jax.random.fold_in(key, 11)
    noise_key, scale_key, offset_key = jax.random.split(key, 3)
    noise = jnp.clip(jax.random.normal(noise_key, (C, N, N), jnp.float32), -5.0, 5.0)
    scales = jnp.exp(jax.random.uniform(scale_key, (1, N, N), jnp.float32, math.log(0.3), math.log(3.0)))
    offsets = jax.random.uniform(offset_key, (1, N, N), jnp.float32, -1.5, 1.5)
    return (scales * (noise + offsets)).astype(jnp.bfloat16)


def shard_levels(key, extent, cuts, smallest, high):
    level = 1.0
    for axis_at, blocks in cuts:
        steps = jax.random.uniform(jax.random.fold_in(jax.random.fold_in(key, 6), axis_at), (blocks,), jnp.float32, smallest / len(cuts), high / len(cuts))
        level = level * jnp.repeat(jnp.exp(steps), extent[axis_at] // blocks).reshape((-1,) + (1,) * (len(extent) - 1 - axis_at))
    return level


def gaussian(rng, extent, spread, limit, cuts=(), kind=jnp.bfloat16):
    factor_of = shard_levels(rng, extent, cuts, -0.22, 0.18) if cuts else 1.0
    array = jax.random.normal(rng, extent, jnp.float32) * spread * factor_of
    return jnp.minimum(jnp.maximum(array, -limit), limit).astype(kind)


def setup_inputs(seed: int = 0) -> dict:
    key_of = jax.random.split(jax.random.key(seed), 12)
    return {
        "pair_field": draw_pair_field(jax.random.fold_in(key_of[11], 71), 0),
        "input_gain": jnp.clip(1.0 + 0.1 * jax.random.normal(key_of[1], (C,), jnp.float32), 0.5, 1.5),
        "input_bias": gaussian(key_of[2], (C,), 0.3, 1.2, (), jnp.float32),
        "left_weight": gaussian(key_of[3], (C, CH), C ** -0.5, 0.5, ((1, 4),)),
        "left_gate": gaussian(key_of[4], (C, CH), C ** -0.5, 0.5, ((1, 4),)),
        "right_weight": gaussian(key_of[5], (C, CH), C ** -0.5, 0.5, ((1, 4),)),
        "right_gate": gaussian(key_of[6], (C, CH), C ** -0.5, 0.5, ((1, 4),)),
        "gate_weight": gaussian(key_of[7], (C, C), C ** -0.5, 0.5, ((1, 4),)),
        "output_gain": jnp.clip(1.0 + 0.1 * jax.random.normal(key_of[8], (CH,), jnp.float32), 0.5, 1.5),
        "output_bias": gaussian(key_of[9], (CH,), 0.3, 1.2, (), jnp.float32),
        "final_weight": gaussian(key_of[10], (CH, C), CH ** -0.5, 0.5, ((1, 4),)),
    }


epsilon = 1e-05

def layer_norm(values, gain, bias):
    average = lax.optimization_barrier(jnp.mean(values, axis=0, keepdims=True))
    centred = values - average
    variance = lax.optimization_barrier(jnp.mean(centred * centred, axis=0, keepdims=True))
    return centred * lax.rsqrt(variance + epsilon) * gain[:, None, None] + bias[:, None, None]

def project(normed, weight):
    flat_field = normed.reshape(normed.shape[0], normed.shape[1] * normed.shape[2])
    result = jnp.dot(jnp.transpose(weight), flat_field, preferred_element_type=jnp.float32)
    return result.reshape(weight.shape[1], normed.shape[1], normed.shape[2])

def reference(pair_field, input_gain, input_bias, left_weight, left_gate, right_weight, right_gate, gate_weight, output_gain, output_bias, final_weight):
    normed = layer_norm(pair_field.astype(jnp.float32), input_gain, input_bias).astype(jnp.bfloat16)
    left_factor = (jax.nn.sigmoid(project(normed, left_gate)) * project(normed, left_weight)).astype(jnp.bfloat16)
    right_factor = (jax.nn.sigmoid(project(normed, right_gate)) * project(normed, right_weight)).astype(jnp.bfloat16)
    gating = jax.nn.sigmoid(project(normed, gate_weight)).astype(jnp.bfloat16)
    product = jnp.einsum('cik,cjk->cij', left_factor.astype(jnp.float32), right_factor.astype(jnp.float32), precision=lax.Precision.HIGHEST).astype(jnp.bfloat16)
    hidden_normed = layer_norm(product.astype(jnp.float32), output_gain, output_bias).astype(jnp.bfloat16)
    update = (gating.astype(jnp.float32) * project(hidden_normed, final_weight)).astype(jnp.bfloat16)
    return jnp.swapaxes(update, 1, 2)
```

```python
import jax
import jax.numpy as jnp
from jax import lax
from jax.sharding import PartitionSpec as P

epsilon = 1e-05


def layer_norm(values, gain, bias):
    average = jnp.mean(values, axis=-2, keepdims=True)
    centred = values - average
    variance = jnp.mean(centred * centred, axis=-2, keepdims=True)
    return centred * lax.rsqrt(variance + epsilon) * gain[:, None] + bias[:, None]


def swap(array, step):
    return lax.ppermute(array, "ch", [(s, s ^ step) for s in range(4)])


def place(blocks, mine):
    stacked = jnp.stack(blocks)
    return jnp.stack([lax.dynamic_index_in_dim(stacked, mine ^ t, 0, False) for t in range(4)])


def body(
    pair_field,
    input_gain,
    input_bias,
    left_weight,
    left_gate,
    right_weight,
    right_gate,
    gate_weight,
    output_gain,
    output_bias,
    final_weight,
):
    mine = lax.axis_index("ch")
    core = mine % 2
    everyone = ("row", "ch")
    weights = jnp.concatenate(
        [w.T for w in (left_weight, left_gate, right_weight, right_gate)], axis=1
    )
    late = lax.all_gather(
        jnp.concatenate([gate_weight.T, final_weight.T], axis=1), "ch", axis=0, tiled=True
    )
    field = jnp.swapaxes(pair_field, 0, 1)

    def message(step):
        part = lax.dynamic_slice(field, (2 * (mine ^ step), 0, 0), (2, 32, 512))
        return jnp.concatenate([part.reshape(64, 512), weights], axis=0)

    got = place([message(0)] + [swap(message(t), t) for t in (1, 2, 3)], mine)
    whole = jnp.swapaxes(got[:, :64].reshape(4, 2, 32, 512), 0, 1).reshape(2, 128, 512)
    wide = got[:, 64:].reshape(128, 4, 128)
    normed = layer_norm(whole.astype(jnp.float32), input_gain, input_bias).astype(jnp.bfloat16)

    def project(weight):
        return jnp.einsum("dc,ack->dak", weight, normed, preferred_element_type=jnp.float32)

    left = jax.nn.sigmoid(project(wide[:, 1])) * project(wide[:, 0])
    right = jax.nn.sigmoid(project(wide[:, 3])) * project(wide[:, 2])
    sent = jnp.concatenate(
        [left.reshape(256, 4, 128), right.reshape(256, 4, 128)], axis=1
    ).astype(jnp.bfloat16)
    factors = lax.all_to_all(sent, everyone, 0, 0, tiled=True)
    other = swap(factors[:, :4], 1)
    own = factors[:, :4].reshape(256, 512)
    other = other.reshape(256, 512)
    rows = jnp.stack([jnp.where(core == 0, own, other), jnp.where(core == 0, other, own)], axis=1)
    product = jnp.einsum(
        "jk,ik->ji",
        factors[:, 4:].reshape(256, 512),
        rows.reshape(512, 512),
        preferred_element_type=jnp.float32,
    ).astype(jnp.bfloat16)
    gating = jax.nn.sigmoid(
        jnp.einsum("ec,acj->jae", late[:, :128], normed, preferred_element_type=jnp.float32)
    ).astype(jnp.bfloat16)
    sent = jnp.concatenate([product.reshape(256, 4, 128), gating.reshape(256, 4, 128)], axis=1)
    got = lax.all_to_all(sent, everyone, 0, 0, tiled=True)
    hidden = jnp.swapaxes(got[:, :4].reshape(128, 2, 512), 0, 1)
    normed = layer_norm(hidden.astype(jnp.float32), output_gain, output_bias).astype(jnp.bfloat16)
    update = jnp.einsum("ed,jdi->jei", late[:, 128:], normed, preferred_element_type=jnp.float32)
    gating = got[:, 4:].reshape(256, 2, 2, 128).transpose(1, 3, 0, 2).reshape(2, 128, 512)
    update = (update * gating.astype(jnp.float32)).astype(jnp.bfloat16)

    def part(step):
        return lax.dynamic_slice(update, (0, 32 * (mine ^ step), 0), (2, 32, 512))

    got = place([part(0)] + [swap(part(t), t) for t in (1, 2, 3)], mine)
    return jnp.swapaxes(got.reshape(8, 32, 512), 0, 1)


def solution(mesh):
    placed = (
        P("ch", "row", None),
        P(),
        P(),
        P(None, "ch"),
        P(None, "ch"),
        P(None, "ch"),
        P(None, "ch"),
        P(None, "ch"),
        P(),
        P(),
        P(None, "ch"),
    )
    return jax.shard_map(
        body, mesh=mesh, in_specs=placed, out_specs=P("ch", "row", None), check_vma=False
    )
```

```python
import jax
import jax.numpy as jnp
from jax import lax
from jax.sharding import PartitionSpec as P

epsilon = 1e-05


def layer_norm(values, gain, bias):
    average = jnp.mean(values, axis=-2, keepdims=True)
    centred = values - average
    variance = jnp.mean(centred * centred, axis=-2, keepdims=True)
    return centred * lax.rsqrt(variance + epsilon) * gain[:, None] + bias[:, None]


def swap(array, step):
    return lax.ppermute(array, "ch", [(s, s ^ step) for s in range(4)])


def place(blocks, mine):
    stacked = jnp.stack(blocks)
    return jnp.stack([lax.dynamic_index_in_dim(stacked, mine ^ t, 0, False) for t in range(4)])


def body(
    pair_field,
    input_gain,
    input_bias,
    left_weight,
    left_gate,
    right_weight,
    right_gate,
    gate_weight,
    output_gain,
    output_bias,
    final_weight,
):
    mine = lax.axis_index("ch")
    core = mine % 2
    everyone = ("row", "ch")
    weights = jnp.concatenate(
        [
            w.T
            for w in (left_weight, left_gate, right_weight, right_gate, gate_weight, final_weight)
        ],
        axis=1,
    )
    wide = place([weights] + [swap(weights, t) for t in (1, 2, 3)], mine).reshape(128, 6, 128)
    field = jnp.swapaxes(pair_field, 0, 1)

    def message(step):
        return lax.dynamic_slice(field, (2 * (mine ^ step), 0, 0), (2, 32, 512))

    got = place([message(0)] + [swap(message(t), t) for t in (1, 2, 3)], mine)
    whole = jnp.swapaxes(got, 0, 1).reshape(2, 128, 512)
    normed = layer_norm(whole.astype(jnp.float32), input_gain, input_bias).astype(jnp.bfloat16)

    def project(weight):
        return jnp.einsum("dc,ack->dak", weight, normed, preferred_element_type=jnp.float32)

    left = jax.nn.sigmoid(project(wide[:, 1])) * project(wide[:, 0])
    right = jax.nn.sigmoid(project(wide[:, 3])) * project(wide[:, 2])
    sent = jnp.concatenate(
        [left.reshape(256, 4, 128), right.reshape(256, 4, 128)], axis=1
    ).astype(jnp.bfloat16)
    factors = lax.all_to_all(sent, everyone, 0, 0, tiled=True)
    other = swap(factors[:, :4], 1)
    own = factors[:, :4].reshape(256, 512)
    other = other.reshape(256, 512)
    rows = jnp.stack([jnp.where(core == 0, own, other), jnp.where(core == 0, other, own)], axis=1)
    product = jnp.einsum(
        "jk,ik->ji",
        factors[:, 4:].reshape(256, 512),
        rows.reshape(512, 512),
        preferred_element_type=jnp.float32,
    ).astype(jnp.bfloat16)
    gating = jax.nn.sigmoid(
        jnp.einsum("ec,acj->jae", wide[:, 4], normed, preferred_element_type=jnp.float32)
    ).astype(jnp.bfloat16)
    gating = lax.all_to_all(gating.reshape(256, 4, 128), everyone, 0, 0, tiled=True)
    got = lax.all_to_all(product.reshape(256, 4, 128), everyone, 0, 0, tiled=True)
    hidden = jnp.swapaxes(got.reshape(128, 2, 512), 0, 1)
    normed = layer_norm(hidden.astype(jnp.float32), output_gain, output_bias).astype(jnp.bfloat16)
    update = jnp.einsum("ed,jdi->jei", wide[:, 5], normed, preferred_element_type=jnp.float32)
    gating = gating.reshape(256, 2, 2, 128).transpose(1, 3, 0, 2).reshape(2, 128, 512)
    update = (update * gating.astype(jnp.float32)).astype(jnp.bfloat16)

    def part(step):
        return lax.dynamic_slice(update, (0, 32 * (mine ^ step), 0), (2, 32, 512))

    got = place([part(0)] + [swap(part(t), t) for t in (1, 2, 3)], mine)
    return jnp.swapaxes(got.reshape(8, 32, 512), 0, 1)


def solution(mesh):
    placed = (
        P("ch", "row", None),
        P(),
        P(),
        P(None, "ch"),
        P(None, "ch"),
        P(None, "ch"),
        P(None, "ch"),
        P(None, "ch"),
        P(),
        P(),
        P(None, "ch"),
    )
    return jax.shard_map(
        body, mesh=mesh, in_specs=placed, out_specs=P("ch", "row", None), check_vma=False
    )
```

```python
import jax
import jax.numpy as jnp
from jax import lax
from jax.experimental import pallas as pl
from jax.experimental.pallas import tpu as pltpu
from jax.sharding import PartitionSpec as P

epsilon = 1e-05
bf16, f32 = jnp.bfloat16, jnp.float32
vmem_bytes = 48 * 1024 * 1024


def call(kernel, name, outs, scratch, flops=0, work=1 << 20):
    return pl.pallas_call(
        kernel,
        name=name,
        out_shape=outs,
        scratch_shapes=scratch,
        compiler_params=pltpu.CompilerParams(vmem_limit_bytes=vmem_bytes),
        cost_estimate=pl.CostEstimate(flops=flops, bytes_accessed=work, transcendentals=0),
    )


def shape(*dims):
    return jax.ShapeDtypeStruct(dims, bf16)


def layer_norm(values, gain, bias):
    average = jnp.mean(values, axis=0, keepdims=True)
    centred = values - average
    variance = jnp.mean(centred * centred, axis=0, keepdims=True)
    wide = values.shape[1] // 128
    return centred * lax.rsqrt(variance + epsilon) * jnp.tile(gain, (1, wide)) + jnp.tile(
        bias, (1, wide)
    )


def column(row):
    return jnp.broadcast_to(row, (128, 128)).T


def lay_out(field, lw, lg, rw, rg, gw, fw, out0, out1, out2, out3, rows):
    mine = lax.axis_index("ch")
    for lane in range(4):
        rows[lane] = field[:, :, 128 * lane : 128 * (lane + 1)].astype(f32).reshape(256, 128)
    for step, out in enumerate((out0, out1, out2, out3)):
        for lane in range(4):
            at = slice(128 * lane, 128 * (lane + 1))
            for ii in range(2):
                out[32 * ii : 32 * (ii + 1), at] = rows[
                    lane, pl.ds(2 * (mine ^ step) + ii, 32, stride=8), :
                ].astype(bf16)
            out[64:96, at] = (lw, lg, rw, rg)[lane][...]
            out[96:112, at] = (gw, fw)[lane % 2][16 * (lane // 2) : 16 * (lane // 2 + 1), :]


def factors(in0, in1, in2, in3, gain, bias, out, normed_out, late, field, weights, rows):
    mine = lax.axis_index("ch")
    for step, block in enumerate((in0, in1, in2, in3)):
        first = pl.multiple_of((mine ^ step) * 32, 32)
        for ii in range(2):
            field[ii, pl.ds(first, 32), :] = block[32 * ii : 32 * (ii + 1), :].astype(f32)
        weights[pl.ds(first, 32), :] = block[64:96, :]
        late[pl.ds(first, 16), :] = block[96:112, 0:256]
        late[pl.ds(pl.multiple_of(first + 16, 16), 16), :] = block[96:112, 256:512]
    gains, biases = column(gain[...]), column(bias[...])
    for ii in range(2):
        normed = layer_norm(field[ii], gains, biases).astype(bf16)
        normed_out[ii] = normed

        def project(which):
            return jnp.dot(
                weights[:, 128 * which : 128 * (which + 1)], normed, preferred_element_type=f32
            )

        for side in range(2):
            factor = jax.nn.sigmoid(project(2 * side + 1)) * project(2 * side)
            for lane in range(4):
                rows[pl.ds(8 * ii + 4 * side + lane, 128, stride=16), :] = factor[
                    :, 128 * lane : 128 * (lane + 1)
                ]
    out[...] = rows[...].reshape(256, 8, 128).astype(bf16)


def gates(normed, late, out, rows):
    for ii in range(2):
        value = jax.nn.sigmoid(
            jnp.dot(late[:, 0:128], normed[ii], preferred_element_type=f32)
        )
        rows[...] = value.T
        for jj in range(2):
            out[2 * jj + ii] = rows[pl.ds(jj, 256, stride=2), :].astype(bf16)


def products(own, other, gating, out, mine_rows, other_rows, left, rows):
    core = lax.axis_index("ch") % 2
    mine_rows[...] = own[...].astype(f32).reshape(2048, 128)
    other_rows[...] = other[...].astype(f32).reshape(2048, 128)
    total = None
    for lane in range(4):
        left[lane, pl.ds(core, 256, stride=2), :] = mine_rows[pl.ds(lane, 256, stride=8), :]
        left[lane, pl.ds(1 - core, 256, stride=2), :] = other_rows[pl.ds(lane, 256, stride=8), :]
        right = mine_rows[pl.ds(4 + lane, 256, stride=8), :].astype(bf16)
        part = lax.dot_general(
            right, left[lane].astype(bf16), (((1,), (1,)), ((), ())), preferred_element_type=f32
        )
        total = part if total is None else total + part
    for lane in range(4):
        rows[pl.ds(lane, 256, stride=8), :] = total[:, 128 * lane : 128 * (lane + 1)]
        rows[pl.ds(4 + lane, 256, stride=8), :] = gating[lane].astype(f32)
    out[...] = rows[...].reshape(256, 8, 128).astype(bf16)


def updates(got, late, gain, bias, out0, out1, out2, out3, rows, gate_rows, update):
    mine = lax.axis_index("ch")
    rows[...] = got[...].astype(f32).reshape(2048, 128)
    gains, biases = column(gain[...]), column(bias[...])
    final = late[:, 128:256]
    for jj in range(2):
        for ii in range(2):
            gate_rows[pl.ds(ii, 256, stride=2), :] = rows[
                pl.ds(4 + 2 * jj + ii, 256, stride=8), :
            ]
        gating = gate_rows[...].T
        for lane in range(4):
            hidden = rows[pl.ds(8 * jj + lane, 128, stride=16), :]
            normed = layer_norm(hidden, gains, biases).astype(bf16)
            value = jnp.dot(final, normed, preferred_element_type=f32)
            at = slice(128 * lane, 128 * (lane + 1))
            update[jj, :, at] = (value * gating[:, at]).astype(bf16)
    for step, out in enumerate((out0, out1, out2, out3)):
        out[...] = update[:, pl.ds(pl.multiple_of((mine ^ step) * 32, 32), 32), :]


def arrange(in0, in1, in2, in3, out, rows):
    mine = lax.axis_index("ch")
    for lane in range(4):
        at = slice(128 * lane, 128 * (lane + 1))
        for step, block in enumerate((in0, in1, in2, in3)):
            for jj in range(2):
                rows[lane, pl.ds(2 * (mine ^ step) + jj, 32, stride=8), :] = block[
                    jj, :, at
                ].astype(f32)
        out[:, :, at] = rows[lane].reshape(32, 8, 128).astype(bf16)


def swap(array, step):
    return lax.ppermute(array, "ch", [(s, s ^ step) for s in range(4)])


def exchange(parts):
    return [parts[0]] + [swap(parts[step], step) for step in (1, 2, 3)]


def body(
    pair_field,
    input_gain,
    input_bias,
    left_weight,
    left_gate,
    right_weight,
    right_gate,
    gate_weight,
    output_gain,
    output_bias,
    final_weight,
):
    everyone = ("row", "ch")
    weights = (left_weight, left_gate, right_weight, right_gate, gate_weight, final_weight)
    parts = call(
        lay_out, "lay_out", (shape(112, 512),) * 4, [pltpu.VMEM((4, 256, 128), f32)]
    )(pair_field, *[w.T for w in weights])
    sent, normed, late = call(
        factors,
        "factors",
        (shape(256, 8, 128), shape(2, 128, 512), shape(128, 256)),
        [
            pltpu.VMEM((2, 128, 512), f32),
            pltpu.VMEM((128, 512), bf16),
            pltpu.VMEM((2048, 128), f32),
        ],
    )(*exchange(parts), input_gain.reshape(1, 128), input_bias.reshape(1, 128))
    own = lax.all_to_all(sent, everyone, 0, 0, tiled=True)
    gating = call(
        gates, "gates", shape(4, 256, 128), [pltpu.VMEM((512, 128), f32)], flops=1 << 30
    )(normed, late)
    sent = call(
        products,
        "products",
        shape(256, 8, 128),
        [
            pltpu.VMEM((2048, 128), f32),
            pltpu.VMEM((2048, 128), f32),
            pltpu.VMEM((4, 512, 128), f32),
            pltpu.VMEM((2048, 128), f32),
        ],
    )(own, swap(own, 1), gating)
    got = lax.all_to_all(sent, everyone, 0, 0, tiled=True)
    parts = call(
        updates,
        "updates",
        (shape(2, 32, 512),) * 4,
        [
            pltpu.VMEM((2048, 128), f32),
            pltpu.VMEM((512, 128), f32),
            pltpu.VMEM((2, 128, 512), bf16),
        ],
    )(got, late, output_gain.reshape(1, 128), output_bias.reshape(1, 128))
    return call(arrange, "arrange", shape(32, 8, 512), [pltpu.VMEM((4, 256, 128), f32)])(
        *exchange(parts)
    )


def solution(mesh):
    placed = (
        P("ch", "row", None),
        P(),
        P(),
        P(None, "ch"),
        P(None, "ch"),
        P(None, "ch"),
        P(None, "ch"),
        P(None, "ch"),
        P(),
        P(),
        P(None, "ch"),
    )
    return jax.shard_map(
        body, mesh=mesh, in_specs=placed, out_specs=P("ch", "row", None), check_vma=False
    )
```

```python
import jax
import jax.numpy as jnp
from jax import lax
from jax.experimental import pallas as pl
from jax.experimental.pallas import tpu as pltpu
from jax.sharding import Mesh
from jax.sharding import PartitionSpec as P

epsilon = 1e-05
bf16, f32 = jnp.bfloat16, jnp.float32


def call(kernel, name, outs, scratch, flops=0, work=1 << 20, **more):
    return pl.pallas_call(
        kernel,
        name=name,
        out_shape=outs,
        scratch_shapes=scratch,
        cost_estimate=pl.CostEstimate(flops=flops, bytes_accessed=work, transcendentals=0),
        **more,
    )


def shape(*dims):
    return jax.ShapeDtypeStruct(dims, bf16)


def layer_norm(values, gain, bias):
    average = jnp.mean(values, axis=0, keepdims=True)
    centred = values - average
    variance = jnp.mean(centred * centred, axis=0, keepdims=True)
    wide = values.shape[1] // 128
    return centred * lax.rsqrt(variance + epsilon) * jnp.tile(gain, (1, wide)) + jnp.tile(
        bias, (1, wide)
    )


def column(row):
    return jnp.broadcast_to(row, (128, 128)).T


def position():
    return 2 * lax.axis_index("xl") + lax.axis_index("core")


def lay_out(*refs):
    sources, outs, vectors = refs[:11], refs[11:15], refs[15]
    field, weights, rows, semaphores = refs[16:]
    copies = [
        pltpu.make_async_copy(source, target, semaphores.at[at])
        for at, (source, target) in enumerate(
            zip(
                sources,
                [field]
                + [weights.at[w] for w in range(6)]
                + [vectors.at[pl.ds(v, 1)] for v in range(4)],
            )
        )
    ]
    for copy in copies:
        copy.start()
    for copy in copies:
        copy.wait()
    mine = position()
    for lane in range(4):
        rows[lane] = field[:, :, 128 * lane : 128 * (lane + 1)].astype(f32).reshape(256, 128)
    for step, out in enumerate(outs):
        for lane in range(4):
            at = slice(128 * lane, 128 * (lane + 1))
            for ii in range(2):
                out[32 * ii : 32 * (ii + 1), at] = rows[
                    lane, pl.ds(2 * (mine ^ step) + ii, 32, stride=8), :
                ].astype(bf16)
            out[64:96, at] = weights[lane]
            out[96:112, at] = weights[4 + lane % 2, 16 * (lane // 2) : 16 * (lane // 2 + 1), :]


def factors(in0, in1, in2, in3, vectors, out, normed_out, late, field, weights, rows):
    mine = position()
    for step, block in enumerate((in0, in1, in2, in3)):
        first = pl.multiple_of((mine ^ step) * 32, 32)
        for ii in range(2):
            field[ii, pl.ds(first, 32), :] = block[32 * ii : 32 * (ii + 1), :].astype(f32)
        weights[pl.ds(first, 32), :] = block[64:96, :]
        late[pl.ds(first, 16), :] = block[96:112, 0:256]
        late[pl.ds(pl.multiple_of(first + 16, 16), 16), :] = block[96:112, 256:512]
    gains, biases = column(vectors[0:1]), column(vectors[1:2])
    for ii in range(2):
        normed = layer_norm(field[ii], gains, biases).astype(bf16)
        normed_out[ii] = normed

        def project(which):
            return jnp.dot(
                weights[:, 128 * which : 128 * (which + 1)], normed, preferred_element_type=f32
            )

        for side in range(2):
            factor = jax.nn.sigmoid(project(2 * side + 1)) * project(2 * side)
            for lane in range(4):
                rows[pl.ds(8 * side + 4 * ii + lane, 128, stride=16), :] = factor[
                    :, 128 * lane : 128 * (lane + 1)
                ]
    out[...] = rows[...].reshape(128, 16, 128).astype(bf16)


def gates(normed, late, kept, given, rows):
    core = lax.axis_index("core")
    for ii in range(2):
        value = jax.nn.sigmoid(
            jnp.dot(late[:, 0:128], normed[ii], preferred_element_type=f32)
        )
        rows[...] = value.T
        for jj in range(2):
            kept[2 * ii + jj] = rows[pl.ds(2 * core + jj, 128, stride=4), :].astype(bf16)
            given[2 * ii + jj] = rows[pl.ds(2 * (1 - core) + jj, 128, stride=4), :].astype(bf16)


def products(own, other, kept, given, out, mine_rows, other_rows, left, rows):
    core = lax.axis_index("core")
    mine_rows[...] = own[...].astype(f32).reshape(2048, 128)
    other_rows[...] = other[...].astype(f32).reshape(1024, 128)
    total = None
    for lane in range(4):
        for ii in range(2):
            left[lane, pl.ds(2 * core + ii, 128, stride=4), :] = mine_rows[
                pl.ds(4 * ii + lane, 128, stride=16), :
            ]
            left[lane, pl.ds(2 * (1 - core) + ii, 128, stride=4), :] = other_rows[
                pl.ds(4 * ii + lane, 128, stride=8), :
            ]
        right = jnp.concatenate(
            [mine_rows[pl.ds(8 + 4 * jj + lane, 128, stride=16), :] for jj in range(2)], axis=0
        ).astype(bf16)
        part = lax.dot_general(
            right, left[lane].astype(bf16), (((1,), (1,)), ((), ())), preferred_element_type=f32
        )
        total = part if total is None else total + part
    for jj in range(2):
        for lane in range(4):
            rows[pl.ds(4 * jj + lane, 128, stride=16), :] = total[
                128 * jj : 128 * (jj + 1), 128 * lane : 128 * (lane + 1)
            ]
        for ii in range(2):
            at = 8 + 4 * jj + ii
            rows[pl.ds(at + 2 * core, 128, stride=16), :] = kept[2 * ii + jj].astype(f32)
            rows[pl.ds(at + 2 * (1 - core), 128, stride=16), :] = given[2 * ii + jj].astype(f32)
    out[...] = rows[...].reshape(128, 16, 128).astype(bf16)


def updates(got, late, vectors, out0, out1, out2, out3, rows, gate_rows, update):
    mine = position()
    rows[...] = got[...].astype(f32).reshape(2048, 128)
    gains, biases = column(vectors[2:3]), column(vectors[3:4])
    final = late[:, 128:256]
    for jj in range(2):
        for ii in range(4):
            gate_rows[pl.ds(ii, 128, stride=4), :] = rows[
                pl.ds(8 + 4 * jj + ii, 128, stride=16), :
            ]
        gating = gate_rows[...].T
        for lane in range(4):
            hidden = rows[pl.ds(4 * jj + lane, 128, stride=16), :]
            normed = layer_norm(hidden, gains, biases).astype(bf16)
            value = jnp.dot(final, normed, preferred_element_type=f32)
            at = slice(128 * lane, 128 * (lane + 1))
            update[jj, :, at] = (value * gating[:, at]).astype(bf16)
    for step, out in enumerate((out0, out1, out2, out3)):
        out[...] = update[:, pl.ds(pl.multiple_of((mine ^ step) * 32, 32), 32), :]


def arrange(in0, in1, in2, in3, out, rows):
    mine = position()
    for lane in range(4):
        at = slice(128 * lane, 128 * (lane + 1))
        for step, block in enumerate((in0, in1, in2, in3)):
            for jj in range(2):
                rows[lane, pl.ds(2 * (mine ^ step) + jj, 32, stride=8), :] = block[
                    jj, :, at
                ].astype(f32)
        out[:, :, at] = rows[lane].reshape(32, 8, 128).astype(bf16)


def swap(array, step):
    return lax.ppermute(array, ("xl", "core"), [(s, s ^ step) for s in range(4)])


def exchange(parts):
    return [parts[0]] + [swap(parts[step], step) for step in (1, 2, 3)]


def body(
    pair_field,
    input_gain,
    input_bias,
    left_weight,
    left_gate,
    right_weight,
    right_gate,
    gate_weight,
    output_gain,
    output_bias,
    final_weight,
):
    same_core = ("row", "xl")
    weights = (left_weight, left_gate, right_weight, right_gate, gate_weight, final_weight)
    vectors = (input_gain, input_bias, output_gain, output_bias)
    *parts, vectors = call(
        lay_out,
        "lay_out",
        (shape(112, 512),) * 4 + (jax.ShapeDtypeStruct((4, 128), f32),),
        [
            pltpu.VMEM((32, 8, 512), bf16),
            pltpu.VMEM((6, 32, 128), bf16),
            pltpu.VMEM((4, 256, 128), f32),
            pltpu.SemaphoreType.DMA((11,)),
        ],
        in_specs=[pl.BlockSpec(memory_space=pl.ANY)] * 11,
    )(pair_field, *[w.T for w in weights], *[v.reshape(1, 128) for v in vectors])
    sent, normed, late = call(
        factors,
        "factors",
        (shape(128, 16, 128), shape(2, 128, 512), shape(128, 256)),
        [
            pltpu.VMEM((2, 128, 512), f32),
            pltpu.VMEM((128, 512), bf16),
            pltpu.VMEM((2048, 128), f32),
        ],
    )(*exchange(parts), vectors)
    own = lax.all_to_all(sent, same_core, 0, 0, tiled=True)
    kept, given = call(
        gates,
        "gates",
        (shape(4, 128, 128),) * 2,
        [pltpu.VMEM((512, 128), f32)],
        flops=1 << 30,
    )(normed, late)
    sent = call(
        products,
        "products",
        shape(128, 16, 128),
        [
            pltpu.VMEM((2048, 128), f32),
            pltpu.VMEM((1024, 128), f32),
            pltpu.VMEM((4, 512, 128), f32),
            pltpu.VMEM((2048, 128), f32),
        ],
    )(own, swap(own[:, :8], 1), kept, swap(given, 1))
    got = lax.all_to_all(sent, same_core, 0, 0, tiled=True)
    parts = call(
        updates,
        "updates",
        (shape(2, 32, 512),) * 4,
        [
            pltpu.VMEM((2048, 128), f32),
            pltpu.VMEM((512, 128), f32),
            pltpu.VMEM((2, 128, 512), bf16),
        ],
    )(got, late, vectors)
    return call(arrange, "arrange", shape(32, 8, 512), [pltpu.VMEM((4, 256, 128), f32)])(
        *exchange(parts)
    )


def solution(mesh):
    mesh = Mesh(mesh.devices.reshape(64, 2, 2), ("row", "xl", "core"))
    ch = ("xl", "core")
    placed = (
        P(ch, "row", None),
        P(),
        P(),
        P(None, ch),
        P(None, ch),
        P(None, ch),
        P(None, ch),
        P(None, ch),
        P(),
        P(),
        P(None, ch),
    )
    return jax.shard_map(
        body, mesh=mesh, in_specs=placed, out_specs=P(ch, "row", None), check_vma=False
    )
```

```python
import jax
import jax.numpy as jnp
from jax import lax
from jax.experimental import pallas as pl
from jax.experimental.pallas import tpu as pltpu
from jax.sharding import Mesh
from jax.sharding import PartitionSpec as P

epsilon = 1e-05
bf16, f32 = jnp.bfloat16, jnp.float32
vmem_bytes = 16 * 1024 * 1024


def call(kernel, name, outs, scratch, flops=0, work=1 << 20, limit=vmem_bytes, **more):
    return pl.pallas_call(
        kernel,
        name=name,
        out_shape=outs,
        scratch_shapes=scratch,
        cost_estimate=pl.CostEstimate(flops=flops, bytes_accessed=work, transcendentals=0),
        compiler_params=pltpu.CompilerParams(vmem_limit_bytes=limit),
        **more,
    )


def shape(*dims):
    return jax.ShapeDtypeStruct(dims, bf16)


def layer_norm(values, gain, bias):
    average = jnp.mean(values, axis=0, keepdims=True)
    centred = values - average
    variance = jnp.mean(centred * centred, axis=0, keepdims=True)
    wide = values.shape[1] // 128
    return centred * lax.rsqrt(variance + epsilon) * jnp.tile(gain, (1, wide)) + jnp.tile(
        bias, (1, wide)
    )


def column(row):
    return jnp.broadcast_to(row, (128, 128)).T


def position():
    return 2 * lax.axis_index("xl") + lax.axis_index("core")


def lay_out(*refs):
    sources, outs, vectors = refs[:11], refs[11:15], refs[15]
    field, weights, rows, semaphores = refs[16:]
    copies = [
        pltpu.make_async_copy(source, target, semaphores.at[at])
        for at, (source, target) in enumerate(
            zip(
                sources,
                [field]
                + [weights.at[w] for w in range(6)]
                + [vectors.at[pl.ds(v, 1)] for v in range(4)],
            )
        )
    ]
    for copy in copies:
        copy.start()
    for copy in copies:
        copy.wait()
    mine = position()
    for lane in range(4):
        rows[lane] = field[:, :, 128 * lane : 128 * (lane + 1)].astype(f32).reshape(256, 128)
    for step, out in enumerate(outs):
        for lane in range(4):
            at = slice(128 * lane, 128 * (lane + 1))
            for ii in range(2):
                out[32 * ii : 32 * (ii + 1), at] = rows[
                    lane, pl.ds(2 * (mine ^ step) + ii, 32, stride=8), :
                ].astype(bf16)
            out[64:96, at] = weights[lane]
            out[96:112, at] = weights[4 + lane % 2, 16 * (lane // 2) : 16 * (lane // 2 + 1), :]


def factors(in0, in1, in2, in3, vectors, out, normed_out, late, field, weights, rows):
    mine = position()
    for step, block in enumerate((in0, in1, in2, in3)):
        first = pl.multiple_of((mine ^ step) * 32, 32)
        for ii in range(2):
            field[ii, pl.ds(first, 32), :] = block[32 * ii : 32 * (ii + 1), :].astype(f32)
        weights[pl.ds(first, 32), :] = block[64:96, :]
        late[pl.ds(first, 16), :] = block[96:112, 0:256]
        late[pl.ds(pl.multiple_of(first + 16, 16), 16), :] = block[96:112, 256:512]
    gains, biases = column(vectors[0:1]), column(vectors[1:2])
    for ii in range(2):
        normed = layer_norm(field[ii], gains, biases).astype(bf16)
        normed_out[ii] = normed

        def project(which):
            return jnp.dot(
                weights[:, 128 * which : 128 * (which + 1)], normed, preferred_element_type=f32
            )

        for side in range(2):
            factor = jax.nn.sigmoid(project(2 * side + 1)) * project(2 * side)
            for lane in range(4):
                rows[pl.ds(8 * side + 4 * ii + lane, 128, stride=16), :] = factor[
                    :, 128 * lane : 128 * (lane + 1)
                ]
    out[...] = rows[...].reshape(128, 16, 128).astype(bf16)


def gates(normed, late, kept, given, rows):
    core = lax.axis_index("core")
    for ii in range(2):
        value = jax.nn.sigmoid(
            jnp.dot(late[:, 0:128], normed[ii], preferred_element_type=f32)
        )
        rows[...] = value.T
        for jj in range(2):
            kept[2 * ii + jj] = rows[pl.ds(2 * core + jj, 128, stride=4), :].astype(bf16)
            given[2 * ii + jj] = rows[pl.ds(2 * (1 - core) + jj, 128, stride=4), :].astype(bf16)


def products(own, other, kept, given, out, mine_rows, other_rows, left, rows):
    core = lax.axis_index("core")
    mine_rows[...] = own[...].astype(f32).reshape(2048, 128)
    other_rows[...] = other[...].astype(f32).reshape(1024, 128)
    total = None
    for lane in range(4):
        for ii in range(2):
            left[lane, pl.ds(2 * core + ii, 128, stride=4), :] = mine_rows[
                pl.ds(4 * ii + lane, 128, stride=16), :
            ]
            left[lane, pl.ds(2 * (1 - core) + ii, 128, stride=4), :] = other_rows[
                pl.ds(4 * ii + lane, 128, stride=8), :
            ]
        right = jnp.concatenate(
            [mine_rows[pl.ds(8 + 4 * jj + lane, 128, stride=16), :] for jj in range(2)], axis=0
        ).astype(bf16)
        part = lax.dot_general(
            right, left[lane].astype(bf16), (((1,), (1,)), ((), ())), preferred_element_type=f32
        )
        total = part if total is None else total + part
    for jj in range(2):
        for lane in range(4):
            rows[pl.ds(4 * jj + lane, 128, stride=16), :] = total[
                128 * jj : 128 * (jj + 1), 128 * lane : 128 * (lane + 1)
            ]
        for ii in range(2):
            at = 8 + 4 * jj + ii
            rows[pl.ds(at + 2 * core, 128, stride=16), :] = kept[2 * ii + jj].astype(f32)
            rows[pl.ds(at + 2 * (1 - core), 128, stride=16), :] = given[2 * ii + jj].astype(f32)
    out[...] = rows[...].reshape(128, 16, 128).astype(bf16)


def updates(got, late, vectors, out0, out1, out2, out3, rows, gate_rows, update):
    mine = position()
    rows[...] = got[...].astype(f32).reshape(2048, 128)
    gains, biases = column(vectors[2:3]), column(vectors[3:4])
    final = late[:, 128:256]
    for jj in range(2):
        for ii in range(4):
            gate_rows[pl.ds(ii, 128, stride=4), :] = rows[
                pl.ds(8 + 4 * jj + ii, 128, stride=16), :
            ]
        gating = gate_rows[...].T
        for lane in range(4):
            hidden = rows[pl.ds(4 * jj + lane, 128, stride=16), :]
            normed = layer_norm(hidden, gains, biases).astype(bf16)
            value = jnp.dot(final, normed, preferred_element_type=f32)
            at = slice(128 * lane, 128 * (lane + 1))
            update[jj, :, at] = (value * gating[:, at]).astype(bf16)
    for step, out in enumerate((out0, out1, out2, out3)):
        out[...] = update[:, pl.ds(pl.multiple_of((mine ^ step) * 32, 32), 32), :]


def arrange(in0, in1, in2, in3, out, rows):
    mine = position()
    for lane in range(4):
        at = slice(128 * lane, 128 * (lane + 1))
        for step, block in enumerate((in0, in1, in2, in3)):
            for jj in range(2):
                rows[lane, pl.ds(2 * (mine ^ step) + jj, 32, stride=8), :] = block[
                    jj, :, at
                ].astype(f32)
        out[:, :, at] = rows[lane].reshape(32, 8, 128).astype(bf16)


def swap(array, step):
    return lax.ppermute(array, ("xl", "core"), [(s, s ^ step) for s in range(4)])


def exchange(parts):
    return [parts[0]] + [swap(parts[step], step) for step in (1, 2, 3)]


def body(
    pair_field,
    input_gain,
    input_bias,
    left_weight,
    left_gate,
    right_weight,
    right_gate,
    gate_weight,
    output_gain,
    output_bias,
    final_weight,
):
    same_core = ("row", "xl")
    weights = (left_weight, left_gate, right_weight, right_gate, gate_weight, final_weight)
    vectors = (input_gain, input_bias, output_gain, output_bias)
    *parts, vectors = call(
        lay_out,
        "lay_out",
        (shape(112, 512),) * 4 + (jax.ShapeDtypeStruct((4, 128), f32),),
        [
            pltpu.VMEM((32, 8, 512), bf16),
            pltpu.VMEM((6, 32, 128), bf16),
            pltpu.VMEM((4, 256, 128), f32),
            pltpu.SemaphoreType.DMA((11,)),
        ],
        limit=60 * 1024 * 1024,
        in_specs=[pl.BlockSpec(memory_space=pltpu.HBM)] * 11,
    )(pair_field, *[w.T for w in weights], *[v.reshape(1, 128) for v in vectors])
    sent, normed, late = call(
        factors,
        "factors",
        (shape(128, 16, 128), shape(2, 128, 512), shape(128, 256)),
        [
            pltpu.VMEM((2, 128, 512), f32),
            pltpu.VMEM((128, 512), bf16),
            pltpu.VMEM((2048, 128), f32),
        ],
    )(*exchange(parts), vectors)
    own = lax.all_to_all(sent, same_core, 0, 0, tiled=True)
    kept, given = call(
        gates,
        "gates",
        (shape(4, 128, 128),) * 2,
        [pltpu.VMEM((512, 128), f32)],
        flops=1 << 30,
    )(normed, late)
    sent = call(
        products,
        "products",
        shape(128, 16, 128),
        [
            pltpu.VMEM((2048, 128), f32),
            pltpu.VMEM((1024, 128), f32),
            pltpu.VMEM((4, 512, 128), f32),
            pltpu.VMEM((2048, 128), f32),
        ],
    )(own, swap(own[:, :8], 1), kept, swap(given, 1))
    got = lax.all_to_all(sent, same_core, 0, 0, tiled=True)
    parts = call(
        updates,
        "updates",
        (shape(2, 32, 512),) * 4,
        [
            pltpu.VMEM((2048, 128), f32),
            pltpu.VMEM((512, 128), f32),
            pltpu.VMEM((2, 128, 512), bf16),
        ],
    )(got, late, vectors)
    return call(arrange, "arrange", shape(32, 8, 512), [pltpu.VMEM((4, 256, 128), f32)])(
        *exchange(parts)
    )


def solution(mesh):
    mesh = Mesh(mesh.devices.reshape(64, 2, 2), ("row", "xl", "core"))
    ch = ("xl", "core")
    placed = (
        P(ch, "row", None),
        P(),
        P(),
        P(None, ch),
        P(None, ch),
        P(None, ch),
        P(None, ch),
        P(None, ch),
        P(),
        P(),
        P(None, ch),
    )
    return jax.shard_map(
        body, mesh=mesh, in_specs=placed, out_specs=P(ch, "row", None), check_vma=False
    )
```

```python
import jax
import jax.numpy as jnp
from jax import lax
from jax.experimental import pallas as pl
from jax.experimental.pallas import tpu as pltpu
from jax.sharding import Mesh
from jax.sharding import PartitionSpec as P

epsilon = 1e-05
bf16, f32 = jnp.bfloat16, jnp.float32
vmem_bytes = 16 * 1024 * 1024


def call(kernel, name, outs, scratch, flops=0, work=1 << 20, limit=vmem_bytes, **more):
    return pl.pallas_call(
        kernel,
        name=name,
        out_shape=outs,
        scratch_shapes=scratch,
        cost_estimate=pl.CostEstimate(flops=flops, bytes_accessed=work, transcendentals=0),
        compiler_params=pltpu.CompilerParams(vmem_limit_bytes=limit),
        **more,
    )


def shape(*dims):
    return jax.ShapeDtypeStruct(dims, bf16)


def layer_norm(values, gain, bias):
    average = jnp.mean(values, axis=0, keepdims=True)
    centred = values - average
    variance = jnp.mean(centred * centred, axis=0, keepdims=True)
    wide = values.shape[1] // 128
    return centred * lax.rsqrt(variance + epsilon) * jnp.tile(gain, (1, wide)) + jnp.tile(
        bias, (1, wide)
    )


def column(row):
    return jnp.broadcast_to(row, (128, 128)).T


def residue_order():
    taken = lax.broadcasted_iota(jnp.int32, (128, 128), 0)
    given = lax.broadcasted_iota(jnp.int32, (128, 128), 1)
    matches = taken == given % 64 // 8 * 16 + given // 64 * 8 + given % 8
    return matches.astype(f32).astype(bf16)


def position():
    return 2 * lax.axis_index("xl") + lax.axis_index("core")


def lay_out(*refs):
    sources, outs, shared, vectors = refs[:11], refs[11:15], refs[15], refs[16]
    field, weights, rows, semaphores = refs[17:]
    copies = [
        pltpu.make_async_copy(source, target, semaphores.at[at])
        for at, (source, target) in enumerate(
            zip(
                sources,
                [field]
                + [weights.at[w] for w in range(6)]
                + [vectors.at[pl.ds(v, 1)] for v in range(4)],
            )
        )
    ]
    for copy in copies:
        copy.start()
    for copy in copies:
        copy.wait()
    mine = position()
    for lane in range(4):
        rows[lane] = field[:, :, 128 * lane : 128 * (lane + 1)].astype(f32).reshape(256, 128)
    for step, out in enumerate(outs):
        for lane in range(4):
            at = slice(128 * lane, 128 * (lane + 1))
            for ii in range(2):
                out[32 * ii : 32 * (ii + 1), at] = rows[
                    lane, pl.ds(2 * (mine ^ step) + ii, 32, stride=8), :
                ].astype(bf16)
    for out, first in ((outs[0], 64), (outs[1], 64), (shared, 0)):
        for lane in range(4):
            at = slice(128 * lane, 128 * (lane + 1))
            out[first : first + 32, at] = weights[lane]
            out[first + 32 : first + 48, at] = weights[
                4 + lane % 2, 16 * (lane // 2) : 16 * (lane // 2 + 1), :
            ]


def factors(in0, in1, in2, in3, shared2, shared3, vectors, out, normed_out, late, field, weights, rows):
    mine = position()
    for step, block in enumerate((in0, in1, in2, in3)):
        first = pl.multiple_of((mine ^ step) * 32, 32)
        for ii in range(2):
            field[ii, pl.ds(first, 32), :] = block[32 * ii : 32 * (ii + 1), :].astype(f32)
        block = (in0.at[64:112], in1.at[64:112], shared2, shared3)[step]
        weights[pl.ds(first, 32), :] = block[0:32, :]
        late[pl.ds(first, 16), :] = block[32:48, 0:256]
        late[pl.ds(pl.multiple_of(first + 16, 16), 16), :] = block[32:48, 256:512]
    gains, biases = column(vectors[0:1]), column(vectors[1:2])
    for ii in range(2):
        normed = layer_norm(field[ii], gains, biases).astype(bf16)
        normed_out[ii] = normed

        def project(which):
            return jnp.dot(
                weights[:, 128 * which : 128 * (which + 1)], normed, preferred_element_type=f32
            )

        for side in range(2):
            factor = jax.nn.sigmoid(project(2 * side + 1)) * project(2 * side)
            for lane in range(4):
                rows[pl.ds(8 * side + 4 * ii + lane, 128, stride=16), :] = factor[
                    :, 128 * lane : 128 * (lane + 1)
                ]
    out[...] = rows[...].reshape(128, 16, 128).astype(bf16)


def gates(normed, late, kept, given, rows):
    core = lax.axis_index("core")
    order = residue_order()
    for ii in range(2):
        value = jax.nn.sigmoid(
            jnp.dot(late[:, 0:128], normed[ii], preferred_element_type=f32)
        ).astype(bf16)
        for lane in range(4):
            at = slice(128 * lane, 128 * (lane + 1))
            rows[at] = lax.dot_general(
                order, value[:, at], (((1,), (1,)), ((), ())), preferred_element_type=f32
            )
        for jj in range(2):
            kept[2 * ii + jj] = rows[pl.ds(2 * core + jj, 128, stride=4), :].astype(bf16)
            given[2 * ii + jj] = rows[pl.ds(2 * (1 - core) + jj, 128, stride=4), :].astype(bf16)


def products(own, other, kept, given, out, mine_rows, other_rows, left, rows):
    core = lax.axis_index("core")
    mine_rows[...] = own[...].astype(f32).reshape(2048, 128)
    other_rows[...] = other[...].astype(f32).reshape(1024, 128)
    total = None
    for lane in range(4):
        for ii in range(2):
            left[lane, pl.ds(2 * core + ii, 128, stride=4), :] = mine_rows[
                pl.ds(4 * ii + lane, 128, stride=16), :
            ]
            left[lane, pl.ds(2 * (1 - core) + ii, 128, stride=4), :] = other_rows[
                pl.ds(4 * ii + lane, 128, stride=8), :
            ]
        right = jnp.concatenate(
            [mine_rows[pl.ds(8 + 4 * jj + lane, 128, stride=16), :] for jj in range(2)], axis=0
        ).astype(bf16)
        part = lax.dot_general(
            right, left[lane].astype(bf16), (((1,), (1,)), ((), ())), preferred_element_type=f32
        )
        total = part if total is None else total + part
    for jj in range(2):
        for lane in range(4):
            rows[pl.ds(4 * jj + lane, 128, stride=16), :] = total[
                128 * jj : 128 * (jj + 1), 128 * lane : 128 * (lane + 1)
            ]
        for ii in range(2):
            at = 8 + 4 * jj + ii
            rows[pl.ds(at + 2 * core, 128, stride=16), :] = kept[2 * ii + jj].astype(f32)
            rows[pl.ds(at + 2 * (1 - core), 128, stride=16), :] = given[2 * ii + jj].astype(f32)
    out[...] = rows[...].reshape(128, 16, 128).astype(bf16)


def updates(got, late, vectors, out0, out1, out2, out3, rows, gate_rows, update):
    mine = position()
    rows[...] = got[...].astype(f32).reshape(2048, 128)
    gains, biases = column(vectors[2:3]), column(vectors[3:4])
    final = late[:, 128:256]
    for jj in range(2):
        for ii in range(4):
            gate_rows[pl.ds(ii, 128, stride=4), :] = rows[
                pl.ds(8 + 4 * jj + ii, 128, stride=16), :
            ]
        gating = gate_rows[...].T
        for lane in range(4):
            hidden = rows[pl.ds(4 * jj + lane, 128, stride=16), :]
            normed = layer_norm(hidden, gains, biases).astype(bf16)
            value = jnp.dot(final, normed, preferred_element_type=f32)
            at = slice(128 * lane, 128 * (lane + 1))
            update[jj, :, at] = (value * gating[:, at]).astype(bf16)
    for step, out in enumerate((out0, out1, out2, out3)):
        out[...] = update[:, pl.ds(pl.multiple_of((mine ^ step) * 32, 32), 32), :]


def arrange(in0, in1, in2, in3, out, rows):
    mine = position()
    order = residue_order()
    for lane in range(4):
        at = slice(128 * lane, 128 * (lane + 1))
        for step, block in enumerate((in0, in1, in2, in3)):
            for jj in range(2):
                rows[lane, pl.ds(2 * (mine ^ step) + jj, 32, stride=8), :] = block[
                    jj, :, at
                ].astype(f32)
        placed = jnp.dot(rows[lane].astype(bf16), order, preferred_element_type=f32)
        out[:, :, at] = placed.reshape(32, 8, 128).astype(bf16)


def swap(array, step):
    return lax.ppermute(array, ("xl", "core"), [(s, s ^ step) for s in range(4)])


def around(array, step):
    pairs = [(s, s ^ (4 + step)) for s in range(8)]
    return lax.ppermute(array, ("xh", "xl", "core"), pairs)


def exchange(parts):
    return [parts[0]] + [swap(parts[step], step) for step in (1, 2, 3)]


def body(
    pair_field,
    input_gain,
    input_bias,
    left_weight,
    left_gate,
    right_weight,
    right_gate,
    gate_weight,
    output_gain,
    output_bias,
    final_weight,
):
    same_core = ("y", "z", "xh", "xl")
    weights = (left_weight, left_gate, right_weight, right_gate, gate_weight, final_weight)
    vectors = (input_gain, input_bias, output_gain, output_bias)
    *parts, shared, vectors = call(
        lay_out,
        "lay_out",
        tuple(pltpu.VMEM((high, 512), bf16) for high in (112, 112, 64, 64, 48))
        + (pltpu.VMEM((4, 128), f32),),
        [
            pltpu.VMEM((32, 8, 512), bf16),
            pltpu.VMEM((6, 32, 128), bf16),
            pltpu.VMEM((4, 256, 128), f32),
            pltpu.SemaphoreType.DMA((11,)),
        ],
        limit=60 * 1024 * 1024,
        in_specs=[pl.BlockSpec(memory_space=pltpu.HBM)] * 11,
    )(pair_field, *[w.T for w in weights], *[v.reshape(1, 128) for v in vectors])
    sent, normed, late = call(
        factors,
        "factors",
        (shape(128, 16, 128), shape(2, 128, 512), shape(128, 256)),
        [
            pltpu.VMEM((2, 128, 512), f32),
            pltpu.VMEM((128, 512), bf16),
            pltpu.VMEM((2048, 128), f32),
        ],
    )(*exchange(parts), around(shared, 2), around(shared, 3), vectors)
    own = lax.all_to_all(sent, same_core, 0, 0, tiled=True)
    kept, given = call(
        gates,
        "gates",
        (shape(4, 128, 128),) * 2,
        [pltpu.VMEM((512, 128), f32)],
        flops=1 << 30,
    )(normed, late)
    sent = call(
        products,
        "products",
        shape(128, 16, 128),
        [
            pltpu.VMEM((2048, 128), f32),
            pltpu.VMEM((1024, 128), f32),
            pltpu.VMEM((4, 512, 128), f32),
            pltpu.VMEM((2048, 128), f32),
        ],
    )(own, swap(own[:, :8], 1), kept, swap(given, 1))
    got = lax.all_to_all(sent, same_core, 0, 0, tiled=True)
    parts = call(
        updates,
        "updates",
        (shape(2, 32, 512),) * 4,
        [
            pltpu.VMEM((2048, 128), f32),
            pltpu.VMEM((512, 128), f32),
            pltpu.VMEM((2, 128, 512), bf16),
        ],
    )(got, late, vectors)
    return call(arrange, "arrange", shape(32, 8, 512), [pltpu.VMEM((4, 256, 128), f32)])(
        *exchange(parts)
    )


def solution(mesh):
    mesh = Mesh(mesh.devices.reshape(4, 2, 8, 2, 2), ("y", "xh", "z", "xl", "core"))
    row, ch = ("y", "xh", "z"), ("xl", "core")
    placed = (
        P(ch, row, None),
        P(),
        P(),
        P(None, ch),
        P(None, ch),
        P(None, ch),
        P(None, ch),
        P(None, ch),
        P(),
        P(),
        P(None, ch),
    )
    return jax.shard_map(
        body, mesh=mesh, in_specs=placed, out_specs=P(ch, row, None), check_vma=False
    )
```

```python
import jax
import jax.numpy as jnp
from jax import lax
from jax.experimental import pallas as pl
from jax.experimental.pallas import tpu as pltpu
from jax.sharding import Mesh
from jax.sharding import PartitionSpec as P

epsilon = 1e-05
bf16, f32 = jnp.bfloat16, jnp.float32
vmem_bytes = 16 * 1024 * 1024


def call(kernel, name, outs, scratch, flops=0, work=1 << 20, limit=vmem_bytes, **more):
    return pl.pallas_call(
        kernel,
        name=name,
        out_shape=outs,
        scratch_shapes=scratch,
        cost_estimate=pl.CostEstimate(flops=flops, bytes_accessed=work, transcendentals=0),
        compiler_params=pltpu.CompilerParams(vmem_limit_bytes=limit),
        **more,
    )


def shape(*dims):
    return jax.ShapeDtypeStruct(dims, bf16)


def layer_norm(values, gain, bias):
    average = jnp.mean(values, axis=0, keepdims=True)
    centred = values - average
    variance = jnp.mean(centred * centred, axis=0, keepdims=True)
    wide = values.shape[1] // 128
    return centred * lax.rsqrt(variance + epsilon) * jnp.tile(gain, (1, wide)) + jnp.tile(
        bias, (1, wide)
    )


def column(row):
    return jnp.broadcast_to(row, (128, 128)).T


def residue_order():
    taken = lax.broadcasted_iota(jnp.int32, (128, 128), 0)
    given = lax.broadcasted_iota(jnp.int32, (128, 128), 1)
    matches = taken == given % 64 // 8 * 16 + given // 64 * 8 + given % 8
    return matches.astype(f32).astype(bf16)


def position():
    return 2 * lax.axis_index("xl") + lax.axis_index("core")


def residue(i):
    return slice(32 * i + 48 * (i // 4), 32 * (i + 1) + 48 * (i // 4))


def lay_out(*refs):
    sources, (whole, vectors) = refs[:11], refs[11:13]
    field, weights, rows, semaphores = refs[13:]
    copies = [
        pltpu.make_async_copy(source, target, semaphores.at[at])
        for at, (source, target) in enumerate(
            zip(
                sources,
                [field]
                + [weights.at[w] for w in range(6)]
                + [vectors.at[pl.ds(v, 1)] for v in range(4)],
            )
        )
    ]
    for copy in copies:
        copy.start()
    for copy in copies:
        copy.wait()
    for lane in range(4):
        at = slice(128 * lane, 128 * (lane + 1))
        rows[lane] = field[:, :, at].astype(f32).reshape(256, 128)
        for i in range(8):
            whole[residue(i), at] = rows[lane, pl.ds(i, 32, stride=8), :].astype(bf16)
        whole[128:160, at] = weights[lane]
        whole[160:176, at] = weights[4 + lane % 2, 16 * (lane // 2) : 16 * (lane // 2 + 1), :]


def scatter_field(own, mate, out, field, columns, rows):
    order = residue_order()
    for i in range(8):
        field[64 * i : 64 * i + 32, :] = mate[residue(i), :]
        field[64 * i + 32 : 64 * (i + 1), :] = own[residue(i), :]
    for group in range(4):
        for block in range(4):
            at = slice(128 * block, 128 * (block + 1))
            columns[at] = lax.dot_general(
                order,
                field[128 * group : 128 * (group + 1), at],
                (((1,), (1,)), ((), ())),
                preferred_element_type=f32,
            )
        for jj in range(4):
            rows[pl.ds(4 * jj + group, 128, stride=16), :] = columns[pl.ds(jj, 128, stride=4), :]
    out[...] = rows[...].reshape(128, 16, 128).astype(bf16)


def gather_field(got, vectors, out, rows, columns):
    rows[...] = got[...].astype(f32).reshape(2048, 128)
    gains, biases = column(vectors[0:1]), column(vectors[1:2])
    low = lax.broadcasted_iota(jnp.int32, (64, 128), 1) < 64
    for jj in range(4):
        for group in range(4):
            near = rows[pl.ds(4 * jj + group, 64, stride=32), :]
            far = rows[pl.ds(16 + 4 * jj + group, 64, stride=32), :]
            columns[pl.ds(2 * group, 64, stride=8), :] = jnp.where(
                low, near, pltpu.roll(far, 64, 1)
            )
            columns[pl.ds(2 * group + 1, 64, stride=8), :] = jnp.where(
                low, pltpu.roll(near, 64, 1), far
            )
        out[jj] = layer_norm(columns[...].T, gains, biases).astype(bf16)


def factors(own, mate, own_far, mate_far, vectors, out, late, field, weights, rows):
    mine, chip = position(), lax.axis_index("xl")
    for step, block in enumerate((own, mate, own_far, mate_far)):
        first = pl.multiple_of((mine ^ step) * 32, 32)
        start = pl.multiple_of(176 * chip if step < 2 else 48 * chip, 16)
        for ii in range(4):
            field[ii, pl.ds(first, 32), :] = block[
                pl.ds(pl.multiple_of(start + 32 * ii, 16), 32), :
            ].astype(f32)
        start = 128 if step < 2 else pl.multiple_of(128 * (1 - chip), 128)
        weights[pl.ds(first, 32), :] = block[pl.ds(start, 32), :]
        after = block[pl.ds(start + 32, 16), :]
        late[pl.ds(first, 16), :] = after[:, 0:256]
        late[pl.ds(pl.multiple_of(first + 16, 16), 16), :] = after[:, 256:512]
    gains, biases = column(vectors[0:1]), column(vectors[1:2])
    for ii in range(4):
        normed = layer_norm(field[ii], gains, biases).astype(bf16)

        def project(which):
            return jnp.dot(
                weights[:, 128 * which : 128 * (which + 1)], normed, preferred_element_type=f32
            )

        for side in range(2):
            factor = jax.nn.sigmoid(project(2 * side + 1)) * project(2 * side)
            for lane in range(4):
                rows[pl.ds(16 * side + 4 * ii + lane, 128, stride=32), :] = factor[
                    :, 128 * lane : 128 * (lane + 1)
                ]
    out[...] = rows[...].reshape(128, 32, 128).astype(bf16)


def products(got, out, received, left, right, rows):
    received[...] = got[...].astype(f32).reshape(4096, 128)
    for lane in range(4):
        for ii in range(4):
            left[lane, pl.ds(ii, 128, stride=4), :] = received[
                pl.ds(4 * ii + lane, 128, stride=32), :
            ]
            right[128 * ii : 128 * (ii + 1), 128 * lane : 128 * (lane + 1)] = received[
                pl.ds(16 + 4 * ii + lane, 128, stride=32), :
            ].astype(bf16)
    whole = jnp.concatenate([left[lane].astype(bf16) for lane in range(4)], axis=1)
    for jj in range(4):
        total = lax.dot_general(
            right[128 * jj : 128 * (jj + 1), :],
            whole,
            (((1,), (1,)), ((), ())),
            preferred_element_type=f32,
        )
        for lane in range(4):
            rows[pl.ds(4 * jj + lane, 128, stride=16), :] = total[
                :, 128 * lane : 128 * (lane + 1)
            ]
    out[...] = rows[...].reshape(128, 16, 128).astype(bf16)


def updates(got, normed_field, late, vectors, out0, out1, out2, out3, rows, update):
    mine = position()
    rows[...] = got[...].astype(f32).reshape(2048, 128)
    gains, biases = column(vectors[2:3]), column(vectors[3:4])
    gate, final = late[:, 0:128], late[:, 128:256]
    for jj in range(4):
        gating = jax.nn.sigmoid(
            jnp.dot(gate, normed_field[jj], preferred_element_type=f32)
        ).astype(bf16)
        for lane in range(4):
            hidden = rows[pl.ds(4 * jj + lane, 128, stride=16), :]
            normed = layer_norm(hidden, gains, biases).astype(bf16)
            value = jnp.dot(final, normed, preferred_element_type=f32)
            at = slice(128 * lane, 128 * (lane + 1))
            update[jj, :, at] = (value * gating[:, at].astype(f32)).astype(bf16)
    for step, out in enumerate((out0, out1, out2, out3)):
        out[...] = update[:, pl.ds(pl.multiple_of((mine ^ step) * 32, 32), 32), :]


def arrange(own, in1, in2, in3, out, rows):
    first = lax.axis_index("core") == 0
    near = 4 * lax.axis_index("xl")
    order = residue_order()
    for lane in range(4):
        at = slice(128 * lane, 128 * (lane + 1))
        for jj in range(4):
            rows[lane, pl.ds(near + jj, 32, stride=8), :] = jnp.where(
                first, own[jj, :, at].astype(f32), in1[jj, :, at].astype(f32)
            )
            rows[lane, pl.ds(4 - near + jj, 32, stride=8), :] = jnp.where(
                first, in2[jj, :, at].astype(f32), in3[jj, :, at].astype(f32)
            )
        placed = jnp.dot(rows[lane].astype(bf16), order, preferred_element_type=f32)
        out[:, :, at] = placed.reshape(32, 8, 128).astype(bf16)


def send(array, *pairs):
    return lax.ppermute(array, ("xl", "core"), pairs)


def unused(*outs):
    return call(lambda *refs: None, "unused", outs, [])()


def body(
    pair_field,
    input_gain,
    input_bias,
    left_weight,
    left_gate,
    right_weight,
    right_gate,
    gate_weight,
    output_gain,
    output_bias,
    final_weight,
):
    same_core = ("y", "z", "xh", "xl")
    first = lax.axis_index("core") == 0
    chip = lax.axis_index("xl")
    weights = (left_weight, left_gate, right_weight, right_gate, gate_weight, final_weight)
    vectors = (input_gain, input_bias, output_gain, output_bias)
    whole, vectors = call(
        lay_out,
        "lay_out",
        (
            pltpu.VMEM((304, 512), bf16),
            pltpu.VMEM((4, 128), f32),
        ),
        [
            pltpu.VMEM((32, 8, 512), bf16),
            pltpu.VMEM((6, 32, 128), bf16),
            pltpu.VMEM((4, 256, 128), f32),
            pltpu.SemaphoreType.DMA((11,)),
        ],
        limit=60 * 1024 * 1024,
        in_specs=[pl.BlockSpec(memory_space=pltpu.HBM)] * 11,
    )(pair_field, *[w.T for w in weights], *[v.reshape(1, 128) for v in vectors])
    mate = send(whole, (0, 1), (1, 0), (2, 3), (3, 2))
    own_far, mate_far = (
        send(lax.dynamic_slice(part, (128 * (1 - chip), 0), (176, 512)), (0, 2), (2, 0))
        for part in (whole, mate)
    )

    def move_field(own, mate, vectors):
        sent = call(
            scatter_field,
            "scatter_field",
            shape(128, 16, 128),
            [
                pltpu.VMEM((512, 512), bf16),
                pltpu.VMEM((512, 128), f32),
                pltpu.VMEM((2048, 128), f32),
            ],
        )(own, mate)
        got = lax.all_to_all(sent, same_core, 0, 0, tiled=True)
        return call(
            gather_field,
            "gather_field",
            shape(4, 128, 512),
            [pltpu.VMEM((2048, 128), f32), pltpu.VMEM((512, 128), f32)],
        )(got, vectors)

    def multiply(own, mate, own_far, mate_far, vectors):
        sent, late = call(
            factors,
            "factors",
            (shape(128, 32, 128), shape(128, 256)),
            [
                pltpu.VMEM((4, 128, 512), f32),
                pltpu.VMEM((128, 512), bf16),
                pltpu.VMEM((4096, 128), f32),
            ],
        )(own, mate, own_far, mate_far, vectors)
        got = lax.all_to_all(sent, same_core, 0, 0, tiled=True)
        sent = call(
            products,
            "products",
            shape(128, 16, 128),
            [
                pltpu.VMEM((4096, 128), f32),
                pltpu.VMEM((4, 512, 128), f32),
                pltpu.VMEM((512, 512), bf16),
                pltpu.VMEM((2048, 128), f32),
            ],
        )(got)
        return sent, late

    def exchange(sent):
        return lax.all_to_all(sent, same_core, 0, 0, tiled=True)

    def update(got, normed_field, late, vectors):
        return call(
            updates,
            "updates",
            (shape(4, 32, 512),) * 4,
            [pltpu.VMEM((2048, 128), f32), pltpu.VMEM((4, 128, 512), bf16)],
        )(got, normed_field, late, vectors)

    normed_field = lax.cond(
        first, lambda *_: unused(shape(4, 128, 512))[0], move_field, whole, mate, vectors
    )
    sent, late = lax.cond(
        first,
        multiply,
        lambda *_: unused(shape(128, 16, 128), shape(128, 256)),
        whole,
        mate,
        own_far,
        mate_far,
        vectors,
    )
    normed_field, sent = lax.optimization_barrier((normed_field, sent))
    normed_field = send(normed_field, (1, 0), (3, 2))
    got = lax.cond(first, exchange, lambda _: unused(shape(128, 16, 128))[0], sent)
    parts = lax.cond(
        first,
        update,
        lambda *_: unused(*(shape(4, 32, 512),) * 4),
        got,
        normed_field,
        late,
        vectors,
    )
    return call(arrange, "arrange", shape(32, 8, 512), [pltpu.VMEM((4, 256, 128), f32)])(
        parts[0],
        send(parts[1], (0, 1), (2, 3)),
        send(parts[2], (0, 2), (2, 0)),
        send(parts[3], (0, 3), (2, 1)),
    )


def solution(mesh):
    mesh = Mesh(mesh.devices.reshape(4, 2, 8, 2, 2), ("y", "xh", "z", "xl", "core"))
    row, ch = ("y", "xh", "z"), ("xl", "core")
    placed = (
        P(ch, row, None),
        P(),
        P(),
        P(None, ch),
        P(None, ch),
        P(None, ch),
        P(None, ch),
        P(None, ch),
        P(),
        P(),
        P(None, ch),
    )
    return jax.shard_map(
        body, mesh=mesh, in_specs=placed, out_specs=P(ch, row, None), check_vma=False
    )
```

```python
import jax
import jax.numpy as jnp
import numpy as np
from jax import lax
from jax.experimental import pallas as pl
from jax.experimental.pallas import tpu as pltpu
from jax.sharding import Mesh
from jax.sharding import PartitionSpec as P

epsilon = 1e-05
first_y, first_z, first_x = 2, 5, 2
bf16, f32 = jnp.bfloat16, jnp.float32
vmem_bytes = 16 * 1024 * 1024


def call(kernel, name, outs, scratch, flops=0, work=1 << 20, limit=vmem_bytes, **more):
    return pl.pallas_call(
        kernel,
        name=name,
        out_shape=outs,
        scratch_shapes=scratch,
        cost_estimate=pl.CostEstimate(flops=flops, bytes_accessed=work, transcendentals=0),
        compiler_params=pltpu.CompilerParams(vmem_limit_bytes=limit),
        **more,
    )


def shape(*dims):
    return jax.ShapeDtypeStruct(dims, bf16)


def layer_norm(values, gain, bias):
    average = jnp.mean(values, axis=0, keepdims=True)
    centred = values - average
    variance = jnp.mean(centred * centred, axis=0, keepdims=True)
    wide = values.shape[1] // 128
    return centred * lax.rsqrt(variance + epsilon) * jnp.tile(gain, (1, wide)) + jnp.tile(
        bias, (1, wide)
    )


def column(row):
    return jnp.broadcast_to(row, (128, 128)).T


def peers(core):
    device = np.arange(256).reshape(4, 2, 8, 2, 2)[..., core]
    chips = device.transpose(0, 2, 1, 3).reshape(4, 8, 4)
    chips = np.roll(chips, (-first_y, -first_z, -first_x), (0, 1, 2))
    return chips.reshape(-1).tolist()


def block_of(y):
    at = 128 * ((y - first_y) % 4)
    return slice(at, at + 128)


def residue_order():
    taken = lax.broadcasted_iota(jnp.int32, (128, 128), 0)
    given = lax.broadcasted_iota(jnp.int32, (128, 128), 1)
    z = (given // 8 + 8 - first_z) % 8
    x = (given // 64 * 2 + given // 4 % 2 + 4 - first_x) % 4
    matches = taken == 16 * z + 4 * x + given % 4
    return matches.astype(f32).astype(bf16)


def position():
    return 2 * lax.axis_index("xl") + lax.axis_index("core")


def lay_out(*refs):
    sources, outs, shared, vectors = refs[:11], refs[11:15], refs[15], refs[16]
    field, weights, rows, semaphores = refs[17:]
    copies = [
        pltpu.make_async_copy(source, target, semaphores.at[at])
        for at, (source, target) in enumerate(
            zip(
                sources,
                [field]
                + [weights.at[w] for w in range(6)]
                + [vectors.at[pl.ds(v, 1)] for v in range(4)],
            )
        )
    ]
    for copy in copies:
        copy.start()
    for copy in copies:
        copy.wait()
    mine = position()
    for lane in range(4):
        rows[lane] = field[:, :, 128 * lane : 128 * (lane + 1)].astype(f32).reshape(256, 128)
    for step, out in enumerate(outs):
        for lane in range(4):
            at = slice(128 * lane, 128 * (lane + 1))
            for ii in range(2):
                out[32 * ii : 32 * (ii + 1), at] = rows[
                    lane, pl.ds(2 * (mine ^ step) + ii, 32, stride=8), :
                ].astype(bf16)
    for out, first in ((outs[0], 64), (outs[1], 64), (shared, 0)):
        for lane in range(4):
            at = slice(128 * lane, 128 * (lane + 1))
            out[first : first + 32, at] = weights[lane]
            out[first + 32 : first + 48, at] = weights[
                4 + lane % 2, 16 * (lane // 2) : 16 * (lane // 2 + 1), :
            ]


def factors(in0, in1, in2, in3, shared2, shared3, vectors, out, normed_out, late, field, weights, rows):
    mine = position()
    for step, block in enumerate((in0, in1, in2, in3)):
        first = pl.multiple_of((mine ^ step) * 32, 32)
        for ii in range(2):
            field[ii, pl.ds(first, 32), :] = block[32 * ii : 32 * (ii + 1), :].astype(f32)
        block = (in0.at[64:112], in1.at[64:112], shared2, shared3)[step]
        weights[pl.ds(first, 32), :] = block[0:32, :]
        late[pl.ds(first, 16), :] = block[32:48, 0:256]
        late[pl.ds(pl.multiple_of(first + 16, 16), 16), :] = block[32:48, 256:512]
    gains, biases = column(vectors[0:1]), column(vectors[1:2])
    for ii in range(2):
        normed = layer_norm(field[ii], gains, biases).astype(bf16)
        normed_out[ii] = normed

        def project(which):
            return jnp.dot(
                weights[:, 128 * which : 128 * (which + 1)], normed, preferred_element_type=f32
            )

        for side in range(2):
            factor = jax.nn.sigmoid(project(2 * side + 1)) * project(2 * side)
            for lane in range(4):
                rows[pl.ds(8 * side + 4 * ii + lane, 128, stride=16), :] = factor[
                    :, 128 * lane : 128 * (lane + 1)
                ]
    out[...] = rows[...].reshape(128, 16, 128).astype(bf16)


def gates(normed, late, kept, given, rows):
    core = lax.axis_index("core")
    order = residue_order()
    for ii in range(2):
        value = jax.nn.sigmoid(
            jnp.dot(late[:, 0:128], normed[ii], preferred_element_type=f32)
        ).astype(bf16)
        for lane in range(4):
            at = slice(128 * lane, 128 * (lane + 1))
            rows[block_of(lane)] = lax.dot_general(
                order, value[:, at], (((1,), (1,)), ((), ())), preferred_element_type=f32
            )
        for jj in range(2):
            kept[2 * ii + jj] = rows[pl.ds(2 * core + jj, 128, stride=4), :].astype(bf16)
            given[2 * ii + jj] = rows[pl.ds(2 * (1 - core) + jj, 128, stride=4), :].astype(bf16)


def products(own, other, kept, given, out, mine_rows, other_rows, left, rows):
    core = lax.axis_index("core")
    mine_rows[...] = own[...].astype(f32).reshape(2048, 128)
    other_rows[...] = other[...].astype(f32).reshape(1024, 128)
    total = None
    for lane in range(4):
        for ii in range(2):
            left[lane, pl.ds(2 * core + ii, 128, stride=4), :] = mine_rows[
                pl.ds(4 * ii + lane, 128, stride=16), :
            ]
            left[lane, pl.ds(2 * (1 - core) + ii, 128, stride=4), :] = other_rows[
                pl.ds(4 * ii + lane, 128, stride=8), :
            ]
        right = jnp.concatenate(
            [mine_rows[pl.ds(8 + 4 * jj + lane, 128, stride=16), :] for jj in range(2)], axis=0
        ).astype(bf16)
        part = lax.dot_general(
            right, left[lane].astype(bf16), (((1,), (1,)), ((), ())), preferred_element_type=f32
        )
        total = part if total is None else total + part
    for jj in range(2):
        for lane in range(4):
            rows[pl.ds(4 * jj + lane, 128, stride=16), :] = total[
                128 * jj : 128 * (jj + 1), 128 * lane : 128 * (lane + 1)
            ]
        for ii in range(2):
            at = 8 + 4 * jj + ii
            rows[pl.ds(at + 2 * core, 128, stride=16), :] = kept[2 * ii + jj].astype(f32)
            rows[pl.ds(at + 2 * (1 - core), 128, stride=16), :] = given[2 * ii + jj].astype(f32)
    out[...] = rows[...].reshape(128, 16, 128).astype(bf16)


def updates(got, late, vectors, out0, out1, out2, out3, rows, gate_rows, update):
    mine = position()
    rows[...] = got[...].astype(f32).reshape(2048, 128)
    gains, biases = column(vectors[2:3]), column(vectors[3:4])
    final = late[:, 128:256]
    for jj in range(2):
        for ii in range(4):
            gate_rows[pl.ds(ii, 128, stride=4), :] = rows[
                pl.ds(8 + 4 * jj + ii, 128, stride=16), :
            ]
        gating = gate_rows[...].T
        for lane in range(4):
            hidden = rows[pl.ds(4 * jj + lane, 128, stride=16), :]
            normed = layer_norm(hidden, gains, biases).astype(bf16)
            value = jnp.dot(final, normed, preferred_element_type=f32)
            at = slice(128 * lane, 128 * (lane + 1))
            update[jj, :, at] = (value * gating[:, at]).astype(bf16)
    for step, out in enumerate((out0, out1, out2, out3)):
        out[...] = update[:, pl.ds(pl.multiple_of((mine ^ step) * 32, 32), 32), :]


def arrange(in0, in1, in2, in3, out, rows):
    mine = position()
    order = residue_order()
    natural = {block_of(y).start // 128: slice(128 * y, 128 * (y + 1)) for y in range(4)}
    for lane in range(4):
        at = slice(128 * lane, 128 * (lane + 1))
        for step, block in enumerate((in0, in1, in2, in3)):
            for jj in range(2):
                rows[lane, pl.ds(2 * (mine ^ step) + jj, 32, stride=8), :] = block[
                    jj, :, at
                ].astype(f32)
        placed = jnp.dot(rows[lane].astype(bf16), order, preferred_element_type=f32)
        out[:, :, natural[lane]] = placed.reshape(32, 8, 128).astype(bf16)


def swap(array, step):
    return lax.ppermute(array, ("xl", "core"), [(s, s ^ step) for s in range(4)])


def around(array, step):
    pairs = [(s, s ^ (4 + step)) for s in range(8)]
    return lax.ppermute(array, ("xh", "xl", "core"), pairs)


def scatter(messages):
    return lax.all_to_all(
        messages,
        ("y", "xh", "z", "xl", "core"),
        0,
        0,
        axis_index_groups=[peers(0), peers(1)],
        tiled=True,
    )


def exchange(parts):
    return [parts[0]] + [swap(parts[step], step) for step in (1, 2, 3)]


def body(
    pair_field,
    input_gain,
    input_bias,
    left_weight,
    left_gate,
    right_weight,
    right_gate,
    gate_weight,
    output_gain,
    output_bias,
    final_weight,
):
    weights = (left_weight, left_gate, right_weight, right_gate, gate_weight, final_weight)
    vectors = (input_gain, input_bias, output_gain, output_bias)
    *parts, shared, vectors = call(
        lay_out,
        "lay_out",
        tuple(pltpu.VMEM((high, 512), bf16) for high in (112, 112, 64, 64, 48))
        + (pltpu.VMEM((4, 128), f32),),
        [
            pltpu.VMEM((32, 8, 512), bf16),
            pltpu.VMEM((6, 32, 128), bf16),
            pltpu.VMEM((4, 256, 128), f32),
            pltpu.SemaphoreType.DMA((11,)),
        ],
        limit=60 * 1024 * 1024,
        in_specs=[pl.BlockSpec(memory_space=pltpu.HBM)] * 11,
    )(pair_field, *[w.T for w in weights], *[v.reshape(1, 128) for v in vectors])
    sent, normed, late = call(
        factors,
        "factors",
        (shape(128, 16, 128), shape(2, 128, 512), shape(128, 256)),
        [
            pltpu.VMEM((2, 128, 512), f32),
            pltpu.VMEM((128, 512), bf16),
            pltpu.VMEM((2048, 128), f32),
        ],
    )(*exchange(parts), around(shared, 2), around(shared, 3), vectors)
    own = scatter(sent)
    kept, given = call(
        gates,
        "gates",
        (shape(4, 128, 128),) * 2,
        [pltpu.VMEM((512, 128), f32)],
        flops=1 << 30,
    )(normed, late)
    sent = call(
        products,
        "products",
        shape(128, 16, 128),
        [
            pltpu.VMEM((2048, 128), f32),
            pltpu.VMEM((1024, 128), f32),
            pltpu.VMEM((4, 512, 128), f32),
            pltpu.VMEM((2048, 128), f32),
        ],
    )(own, swap(own[:, :8], 1), kept, swap(given, 1))
    got = scatter(sent)
    parts = call(
        updates,
        "updates",
        (shape(2, 32, 512),) * 4,
        [
            pltpu.VMEM((2048, 128), f32),
            pltpu.VMEM((512, 128), f32),
            pltpu.VMEM((2, 128, 512), bf16),
        ],
    )(got, late, vectors)
    return call(arrange, "arrange", shape(32, 8, 512), [pltpu.VMEM((4, 256, 128), f32)])(
        *exchange(parts)
    )


def solution(mesh):
    mesh = Mesh(mesh.devices.reshape(4, 2, 8, 2, 2), ("y", "xh", "z", "xl", "core"))
    row, ch = ("y", "xh", "z"), ("xl", "core")
    placed = (
        P(ch, row, None),
        P(),
        P(),
        P(None, ch),
        P(None, ch),
        P(None, ch),
        P(None, ch),
        P(None, ch),
        P(),
        P(),
        P(None, ch),
    )
    return jax.shard_map(
        body, mesh=mesh, in_specs=placed, out_specs=P(ch, row, None), check_vma=False
    )
```

```python
import jax
import jax.numpy as jnp
from jax import lax
from jax.experimental import pallas as pl
from jax.experimental.pallas import tpu as pltpu
from jax.sharding import Mesh
from jax.sharding import PartitionSpec as P

epsilon = 1e-05
far_chip = 90
bf16, f32 = jnp.bfloat16, jnp.float32
vmem_bytes = 16 * 1024 * 1024


def call(kernel, name, outs, scratch, flops=0, work=1 << 20, limit=vmem_bytes, **more):
    return pl.pallas_call(
        kernel,
        name=name,
        out_shape=outs,
        scratch_shapes=scratch,
        cost_estimate=pl.CostEstimate(flops=flops, bytes_accessed=work, transcendentals=0),
        compiler_params=pltpu.CompilerParams(vmem_limit_bytes=limit),
        **more,
    )


def shape(*dims):
    return jax.ShapeDtypeStruct(dims, bf16)


def layer_norm(values, gain, bias):
    average = jnp.mean(values, axis=0, keepdims=True)
    centred = values - average
    variance = jnp.mean(centred * centred, axis=0, keepdims=True)
    wide = values.shape[1] // 128
    return centred * lax.rsqrt(variance + epsilon) * jnp.tile(gain, (1, wide)) + jnp.tile(
        bias, (1, wide)
    )


def column(row):
    return jnp.broadcast_to(row, (128, 128)).T


def peers(core):
    devices = list(range(core, 256, 2))
    devices[0], devices[far_chip] = devices[far_chip], devices[0]
    return devices


def restore(rows):
    first, far = slice(0, 4), slice(4 * far_chip, 4 * far_chip + 4)
    kept = rows[first, :]
    rows[first, :] = rows[far, :]
    rows[far, :] = kept


def position():
    return 2 * lax.axis_index("xl") + lax.axis_index("core")


def lay_out(*refs):
    sources, outs, shared, vectors = refs[:11], refs[11:15], refs[15], refs[16]
    field, weights, rows, semaphores = refs[17:]
    copies = [
        pltpu.make_async_copy(source, target, semaphores.at[at])
        for at, (source, target) in enumerate(
            zip(
                sources,
                [field]
                + [weights.at[w] for w in range(6)]
                + [vectors.at[pl.ds(v, 1)] for v in range(4)],
            )
        )
    ]
    for copy in copies:
        copy.start()
    for copy in copies:
        copy.wait()
    mine = position()
    for lane in range(4):
        rows[lane] = field[:, :, 128 * lane : 128 * (lane + 1)].astype(f32).reshape(256, 128)
    for step, out in enumerate(outs):
        for lane in range(4):
            at = slice(128 * lane, 128 * (lane + 1))
            for ii in range(2):
                out[32 * ii : 32 * (ii + 1), at] = rows[
                    lane, pl.ds(2 * (mine ^ step) + ii, 32, stride=8), :
                ].astype(bf16)
    for out, first in ((outs[0], 64), (outs[1], 64), (outs[2], 64), (shared, 0)):
        for lane in range(4):
            at = slice(128 * lane, 128 * (lane + 1))
            out[first : first + 32, at] = weights[lane]
            out[first + 32 : first + 48, at] = weights[
                4 + lane % 2, 16 * (lane // 2) : 16 * (lane // 2 + 1), :
            ]


def factors(in0, in1, in2, in3, shared3, vectors, out, normed_out, late, field, weights, rows):
    mine = position()
    for step, block in enumerate((in0, in1, in2, in3)):
        first = pl.multiple_of((mine ^ step) * 32, 32)
        for ii in range(2):
            field[ii, pl.ds(first, 32), :] = block[32 * ii : 32 * (ii + 1), :].astype(f32)
        block = (in0.at[64:112], in1.at[64:112], in2.at[64:112], shared3)[step]
        weights[pl.ds(first, 32), :] = block[0:32, :]
        late[pl.ds(first, 16), :] = block[32:48, 0:256]
        late[pl.ds(pl.multiple_of(first + 16, 16), 16), :] = block[32:48, 256:512]
    gains, biases = column(vectors[0:1]), column(vectors[1:2])
    for ii in range(2):
        normed = layer_norm(field[ii], gains, biases).astype(bf16)
        normed_out[ii] = normed

        def project(which):
            return jnp.dot(
                weights[:, 128 * which : 128 * (which + 1)], normed, preferred_element_type=f32
            )

        for side in range(2):
            factor = jax.nn.sigmoid(project(2 * side + 1)) * project(2 * side)
            for lane in range(4):
                rows[pl.ds(8 * side + 4 * ii + lane, 128, stride=16), :] = factor[
                    :, 128 * lane : 128 * (lane + 1)
                ]
    out[...] = rows[...].reshape(128, 16, 128).astype(bf16)


def gates(normed, late, kept, given, rows):
    core = lax.axis_index("core")
    for ii in range(2):
        value = jax.nn.sigmoid(jnp.dot(late[:, 0:128], normed[ii], preferred_element_type=f32))
        rows[...] = value.T
        restore(rows)
        for jj in range(2):
            kept[2 * ii + jj] = rows[pl.ds(2 * core + jj, 128, stride=4), :].astype(bf16)
            given[2 * ii + jj] = rows[pl.ds(2 * (1 - core) + jj, 128, stride=4), :].astype(bf16)


def products(own, other, kept, given, out, mine_rows, other_rows, left, rows):
    core = lax.axis_index("core")
    mine_rows[...] = own[...].astype(f32).reshape(2048, 128)
    other_rows[...] = other[...].astype(f32).reshape(1024, 128)
    total = None
    for lane in range(4):
        for ii in range(2):
            left[lane, pl.ds(2 * core + ii, 128, stride=4), :] = mine_rows[
                pl.ds(4 * ii + lane, 128, stride=16), :
            ]
            left[lane, pl.ds(2 * (1 - core) + ii, 128, stride=4), :] = other_rows[
                pl.ds(4 * ii + lane, 128, stride=8), :
            ]
        restore(left.at[lane])
        right = jnp.concatenate(
            [mine_rows[pl.ds(8 + 4 * jj + lane, 128, stride=16), :] for jj in range(2)], axis=0
        ).astype(bf16)
        part = lax.dot_general(
            right, left[lane].astype(bf16), (((1,), (1,)), ((), ())), preferred_element_type=f32
        )
        total = part if total is None else total + part
    for jj in range(2):
        for lane in range(4):
            rows[pl.ds(4 * jj + lane, 128, stride=16), :] = total[
                128 * jj : 128 * (jj + 1), 128 * lane : 128 * (lane + 1)
            ]
        for ii in range(2):
            at = 8 + 4 * jj + ii
            rows[pl.ds(at + 2 * core, 128, stride=16), :] = kept[2 * ii + jj].astype(f32)
            rows[pl.ds(at + 2 * (1 - core), 128, stride=16), :] = given[2 * ii + jj].astype(f32)
    out[...] = rows[...].reshape(128, 16, 128).astype(bf16)


def updates(got, late, vectors, out0, out1, out2, out3, rows, gate_rows, update):
    mine = position()
    rows[...] = got[...].astype(f32).reshape(2048, 128)
    gains, biases = column(vectors[2:3]), column(vectors[3:4])
    final = late[:, 128:256]
    for jj in range(2):
        for ii in range(4):
            gate_rows[pl.ds(ii, 128, stride=4), :] = rows[
                pl.ds(8 + 4 * jj + ii, 128, stride=16), :
            ]
        restore(gate_rows)
        gating = gate_rows[...].T
        for lane in range(4):
            hidden = rows[pl.ds(4 * jj + lane, 128, stride=16), :]
            normed = layer_norm(hidden, gains, biases).astype(bf16)
            value = jnp.dot(final, normed, preferred_element_type=f32)
            at = slice(128 * lane, 128 * (lane + 1))
            update[jj, :, at] = (value * gating[:, at]).astype(bf16)
    for step, out in enumerate((out0, out1, out2, out3)):
        out[...] = update[:, pl.ds(pl.multiple_of((mine ^ step) * 32, 32), 32), :]


def arrange(in0, in1, in2, in3, out, rows):
    mine = position()
    for lane in range(4):
        at = slice(128 * lane, 128 * (lane + 1))
        for step, block in enumerate((in0, in1, in2, in3)):
            for jj in range(2):
                rows[lane, pl.ds(2 * (mine ^ step) + jj, 32, stride=8), :] = block[
                    jj, :, at
                ].astype(f32)
        out[:, :, at] = rows[lane].reshape(32, 8, 128).astype(bf16)


def swap(array, step):
    return lax.ppermute(array, ("xl", "core"), [(s, s ^ step) for s in range(4)])


def around(array, step):
    pairs = [(s, s ^ (4 + step)) for s in range(8)]
    return lax.ppermute(array, ("xh", "xl", "core"), pairs)


def scatter(messages):
    return lax.all_to_all(
        messages,
        ("y", "xh", "z", "xl", "core"),
        0,
        0,
        axis_index_groups=[peers(0), peers(1)],
        tiled=True,
    )


def exchange(parts):
    return [parts[0]] + [swap(parts[step], step) for step in (1, 2, 3)]


def body(
    pair_field,
    input_gain,
    input_bias,
    left_weight,
    left_gate,
    right_weight,
    right_gate,
    gate_weight,
    output_gain,
    output_bias,
    final_weight,
):
    weights = (left_weight, left_gate, right_weight, right_gate, gate_weight, final_weight)
    vectors = (input_gain, input_bias, output_gain, output_bias)
    *parts, shared, vectors = call(
        lay_out,
        "lay_out",
        tuple(pltpu.VMEM((high, 512), bf16) for high in (112, 112, 112, 64, 48))
        + (pltpu.VMEM((4, 128), f32),),
        [
            pltpu.VMEM((32, 8, 512), bf16),
            pltpu.VMEM((6, 32, 128), bf16),
            pltpu.VMEM((4, 256, 128), f32),
            pltpu.SemaphoreType.DMA((11,)),
        ],
        limit=60 * 1024 * 1024,
        in_specs=[pl.BlockSpec(memory_space=pltpu.HBM)] * 11,
    )(pair_field, *[w.T for w in weights], *[v.reshape(1, 128) for v in vectors])
    sent, normed, late = call(
        factors,
        "factors",
        (shape(128, 16, 128), shape(2, 128, 512), shape(128, 256)),
        [
            pltpu.VMEM((2, 128, 512), f32),
            pltpu.VMEM((128, 512), bf16),
            pltpu.VMEM((2048, 128), f32),
        ],
    )(*exchange(parts), around(shared, 3), vectors)
    own = scatter(sent)
    kept, given = call(
        gates,
        "gates",
        (shape(4, 128, 128),) * 2,
        [pltpu.VMEM((512, 128), f32)],
        flops=1 << 30,
    )(normed, late)
    sent = call(
        products,
        "products",
        shape(128, 16, 128),
        [
            pltpu.VMEM((2048, 128), f32),
            pltpu.VMEM((1024, 128), f32),
            pltpu.VMEM((4, 512, 128), f32),
            pltpu.VMEM((2048, 128), f32),
        ],
    )(own, swap(own[:, :8], 1), kept, swap(given, 1))
    got = scatter(sent)
    parts = call(
        updates,
        "updates",
        (shape(2, 32, 512),) * 4,
        [
            pltpu.VMEM((2048, 128), f32),
            pltpu.VMEM((512, 128), f32),
            pltpu.VMEM((2, 128, 512), bf16),
        ],
    )(got, late, vectors)
    return call(arrange, "arrange", shape(32, 8, 512), [pltpu.VMEM((4, 256, 128), f32)])(
        *exchange(parts)
    )


def solution(mesh):
    mesh = Mesh(mesh.devices.reshape(4, 2, 8, 2, 2), ("y", "xh", "z", "xl", "core"))
    row, ch = ("y", "xh", "z"), ("xl", "core")
    placed = (
        P(ch, row, None),
        P(),
        P(),
        P(None, ch),
        P(None, ch),
        P(None, ch),
        P(None, ch),
        P(None, ch),
        P(),
        P(),
        P(None, ch),
    )
    return jax.shard_map(
        body, mesh=mesh, in_specs=placed, out_specs=P(ch, row, None), check_vma=False
    )
```

```python
import jax
import jax.numpy as jnp
from jax import lax
from jax.experimental import pallas as pl
from jax.experimental.pallas import tpu as pltpu
from jax.sharding import Mesh
from jax.sharding import PartitionSpec as P

epsilon = 1e-05
far_pair = 45
bf16, f32 = jnp.bfloat16, jnp.float32
vmem_bytes = 16 * 1024 * 1024


def call(kernel, name, outs, scratch, flops=0, work=1 << 20, limit=vmem_bytes, **more):
    return pl.pallas_call(
        kernel,
        name=name,
        out_shape=outs,
        scratch_shapes=scratch,
        cost_estimate=pl.CostEstimate(flops=flops, bytes_accessed=work, transcendentals=0),
        compiler_params=pltpu.CompilerParams(vmem_limit_bytes=limit),
        **more,
    )


def shape(*dims):
    return jax.ShapeDtypeStruct(dims, bf16)


def layer_norm(values, gain, bias):
    average = jnp.mean(values, axis=0, keepdims=True)
    centred = values - average
    variance = jnp.mean(centred * centred, axis=0, keepdims=True)
    wide = values.shape[1] // 128
    return centred * lax.rsqrt(variance + epsilon) * jnp.tile(gain, (1, wide)) + jnp.tile(
        bias, (1, wide)
    )


def column(row):
    return jnp.broadcast_to(row, (128, 128)).T


def pair_order():
    def distance(pair):
        y, z = pair // 16, pair % 8
        return min(z, 8 - z)

    return [far_pair] + [pair for pair in sorted(range(64), key=distance) if pair != far_pair]


def peers(core):
    return [4 * pair + 2 * xl + core for pair in pair_order() for xl in range(2)]


def to_peers(rows):
    return jnp.concatenate([rows[8 * pair : 8 * pair + 8, :] for pair in pair_order()], axis=0)


def from_peers(rows):
    places = [pair_order().index(pair) for pair in range(64)]
    return jnp.concatenate([rows[8 * place : 8 * place + 8, :] for place in places], axis=0)


def position():
    return 2 * lax.axis_index("xl") + lax.axis_index("core")


def lay_out(*refs):
    sources, outs, shared, vectors = refs[:11], refs[11:15], refs[15], refs[16]
    field, weights, rows, semaphores = refs[17:]
    copies = [
        pltpu.make_async_copy(source, target, semaphores.at[at])
        for at, (source, target) in enumerate(
            zip(
                sources,
                [field]
                + [weights.at[w] for w in range(6)]
                + [vectors.at[pl.ds(v, 1)] for v in range(4)],
            )
        )
    ]
    for copy in copies:
        copy.start()
    for copy in copies:
        copy.wait()
    mine = position()
    for lane in range(4):
        rows[lane] = field[:, :, 128 * lane : 128 * (lane + 1)].astype(f32).reshape(256, 128)
    for step, out in enumerate(outs):
        for lane in range(4):
            at = slice(128 * lane, 128 * (lane + 1))
            for ii in range(2):
                out[32 * ii : 32 * (ii + 1), at] = rows[
                    lane, pl.ds(2 * (mine ^ step) + ii, 32, stride=8), :
                ].astype(bf16)
    for out, first in ((outs[0], 64), (outs[1], 64), (outs[2], 64), (shared, 0)):
        for lane in range(4):
            at = slice(128 * lane, 128 * (lane + 1))
            out[first : first + 32, at] = weights[lane]
            out[first + 32 : first + 48, at] = weights[
                4 + lane % 2, 16 * (lane // 2) : 16 * (lane // 2 + 1), :
            ]


def factors(in0, in1, in2, in3, shared3, vectors, out, normed_out, late, field, weights, rows):
    mine = position()
    for step, block in enumerate((in0, in1, in2, in3)):
        first = pl.multiple_of((mine ^ step) * 32, 32)
        for ii in range(2):
            field[ii, pl.ds(first, 32), :] = block[32 * ii : 32 * (ii + 1), :].astype(f32)
        block = (in0.at[64:112], in1.at[64:112], in2.at[64:112], shared3)[step]
        weights[pl.ds(first, 32), :] = block[0:32, :]
        late[pl.ds(first, 16), :] = block[32:48, 0:256]
        late[pl.ds(pl.multiple_of(first + 16, 16), 16), :] = block[32:48, 256:512]
    gains, biases = column(vectors[0:1]), column(vectors[1:2])
    for ii in range(2):
        normed = layer_norm(field[ii], gains, biases).astype(bf16)
        normed_out[ii] = normed

        def project(which):
            return jnp.dot(
                weights[:, 128 * which : 128 * (which + 1)], normed, preferred_element_type=f32
            )

        for side in range(2):
            factor = jax.nn.sigmoid(project(2 * side + 1)) * project(2 * side)
            for lane in range(4):
                rows[pl.ds(8 * side + 4 * ii + lane, 128, stride=16), :] = factor[
                    :, 128 * lane : 128 * (lane + 1)
                ]
    out[...] = rows[...].reshape(128, 16, 128).astype(bf16)


def gates(normed, late, kept, given, rows):
    core = lax.axis_index("core")
    for ii in range(2):
        value = jax.nn.sigmoid(jnp.dot(late[:, 0:128], normed[ii], preferred_element_type=f32))
        rows[...] = value.T
        rows[...] = to_peers(rows)
        for jj in range(2):
            kept[2 * ii + jj] = rows[pl.ds(2 * core + jj, 128, stride=4), :].astype(bf16)
            given[2 * ii + jj] = rows[pl.ds(2 * (1 - core) + jj, 128, stride=4), :].astype(bf16)


def products(own, other, kept, given, out, mine_rows, other_rows, left, rows):
    core = lax.axis_index("core")
    mine_rows[...] = own[...].astype(f32).reshape(2048, 128)
    other_rows[...] = other[...].astype(f32).reshape(1024, 128)
    total = None
    for lane in range(4):
        for ii in range(2):
            left[lane, pl.ds(2 * core + ii, 128, stride=4), :] = mine_rows[
                pl.ds(4 * ii + lane, 128, stride=16), :
            ]
            left[lane, pl.ds(2 * (1 - core) + ii, 128, stride=4), :] = other_rows[
                pl.ds(4 * ii + lane, 128, stride=8), :
            ]
        right = jnp.concatenate(
            [mine_rows[pl.ds(8 + 4 * jj + lane, 128, stride=16), :] for jj in range(2)], axis=0
        ).astype(bf16)
        part = lax.dot_general(
            right, from_peers(left.at[lane]).astype(bf16), (((1,), (1,)), ((), ())), preferred_element_type=f32
        )
        total = part if total is None else total + part
    for jj in range(2):
        for lane in range(4):
            rows[pl.ds(4 * jj + lane, 128, stride=16), :] = total[
                128 * jj : 128 * (jj + 1), 128 * lane : 128 * (lane + 1)
            ]
        for ii in range(2):
            at = 8 + 4 * jj + ii
            rows[pl.ds(at + 2 * core, 128, stride=16), :] = kept[2 * ii + jj].astype(f32)
            rows[pl.ds(at + 2 * (1 - core), 128, stride=16), :] = given[2 * ii + jj].astype(f32)
    out[...] = rows[...].reshape(128, 16, 128).astype(bf16)


def updates(got, late, vectors, out0, out1, out2, out3, rows, gate_rows, update):
    mine = position()
    rows[...] = got[...].astype(f32).reshape(2048, 128)
    gains, biases = column(vectors[2:3]), column(vectors[3:4])
    final = late[:, 128:256]
    for jj in range(2):
        for ii in range(4):
            gate_rows[pl.ds(ii, 128, stride=4), :] = rows[
                pl.ds(8 + 4 * jj + ii, 128, stride=16), :
            ]
        gating = from_peers(gate_rows).T
        for lane in range(4):
            hidden = rows[pl.ds(4 * jj + lane, 128, stride=16), :]
            normed = layer_norm(hidden, gains, biases).astype(bf16)
            value = jnp.dot(final, normed, preferred_element_type=f32)
            at = slice(128 * lane, 128 * (lane + 1))
            update[jj, :, at] = (value * gating[:, at]).astype(bf16)
    for step, out in enumerate((out0, out1, out2, out3)):
        out[...] = update[:, pl.ds(pl.multiple_of((mine ^ step) * 32, 32), 32), :]


def arrange(in0, in1, in2, in3, out, rows):
    mine = position()
    for lane in range(4):
        at = slice(128 * lane, 128 * (lane + 1))
        for step, block in enumerate((in0, in1, in2, in3)):
            for jj in range(2):
                rows[lane, pl.ds(2 * (mine ^ step) + jj, 32, stride=8), :] = block[
                    jj, :, at
                ].astype(f32)
        out[:, :, at] = rows[lane].reshape(32, 8, 128).astype(bf16)


def swap(array, step):
    return lax.ppermute(array, ("xl", "core"), [(s, s ^ step) for s in range(4)])


def around(array, step):
    pairs = [(s, s ^ (4 + step)) for s in range(8)]
    return lax.ppermute(array, ("xh", "xl", "core"), pairs)


def scatter(messages):
    return lax.all_to_all(
        messages,
        ("y", "xh", "z", "xl", "core"),
        0,
        0,
        axis_index_groups=[peers(0), peers(1)],
        tiled=True,
    )


def exchange(parts):
    return [parts[0]] + [swap(parts[step], step) for step in (1, 2, 3)]


def body(
    pair_field,
    input_gain,
    input_bias,
    left_weight,
    left_gate,
    right_weight,
    right_gate,
    gate_weight,
    output_gain,
    output_bias,
    final_weight,
):
    weights = (left_weight, left_gate, right_weight, right_gate, gate_weight, final_weight)
    vectors = (input_gain, input_bias, output_gain, output_bias)
    *parts, shared, vectors = call(
        lay_out,
        "lay_out",
        tuple(pltpu.VMEM((high, 512), bf16) for high in (112, 112, 112, 64, 48))
        + (pltpu.VMEM((4, 128), f32),),
        [
            pltpu.VMEM((32, 8, 512), bf16),
            pltpu.VMEM((6, 32, 128), bf16),
            pltpu.VMEM((4, 256, 128), f32),
            pltpu.SemaphoreType.DMA((11,)),
        ],
        limit=60 * 1024 * 1024,
        in_specs=[pl.BlockSpec(memory_space=pltpu.HBM)] * 11,
    )(pair_field, *[w.T for w in weights], *[v.reshape(1, 128) for v in vectors])
    sent, normed, late = call(
        factors,
        "factors",
        (shape(128, 16, 128), shape(2, 128, 512), shape(128, 256)),
        [
            pltpu.VMEM((2, 128, 512), f32),
            pltpu.VMEM((128, 512), bf16),
            pltpu.VMEM((2048, 128), f32),
        ],
    )(*exchange(parts), around(shared, 3), vectors)
    own = scatter(sent)
    kept, given = call(
        gates,
        "gates",
        (shape(4, 128, 128),) * 2,
        [pltpu.VMEM((512, 128), f32)],
        flops=1 << 30,
    )(normed, late)
    sent = call(
        products,
        "products",
        shape(128, 16, 128),
        [
            pltpu.VMEM((2048, 128), f32),
            pltpu.VMEM((1024, 128), f32),
            pltpu.VMEM((4, 512, 128), f32),
            pltpu.VMEM((2048, 128), f32),
        ],
    )(own, swap(own[:, :8], 1), kept, swap(given, 1))
    got = scatter(sent)
    parts = call(
        updates,
        "updates",
        (shape(2, 32, 512),) * 4,
        [
            pltpu.VMEM((2048, 128), f32),
            pltpu.VMEM((512, 128), f32),
            pltpu.VMEM((2, 128, 512), bf16),
        ],
    )(got, late, vectors)
    return call(arrange, "arrange", shape(32, 8, 512), [pltpu.VMEM((4, 256, 128), f32)])(
        *exchange(parts)
    )


def solution(mesh):
    mesh = Mesh(mesh.devices.reshape(4, 2, 8, 2, 2), ("y", "xh", "z", "xl", "core"))
    row, ch = ("y", "xh", "z"), ("xl", "core")
    placed = (
        P(ch, row, None),
        P(),
        P(),
        P(None, ch),
        P(None, ch),
        P(None, ch),
        P(None, ch),
        P(None, ch),
        P(),
        P(),
        P(None, ch),
    )
    return jax.shard_map(
        body, mesh=mesh, in_specs=placed, out_specs=P(ch, row, None), check_vma=False
    )
```

```python
import jax
import jax.numpy as jnp
from jax import lax
from jax.experimental import pallas as pl
from jax.experimental.pallas import tpu as pltpu
from jax.sharding import Mesh
from jax.sharding import PartitionSpec as P

epsilon = 1e-05
far_pair = 45
bf16, f32 = jnp.bfloat16, jnp.float32
vmem_bytes = 16 * 1024 * 1024


def call(kernel, name, outs, scratch, flops=0, work=1 << 20, limit=vmem_bytes, **more):
    return pl.pallas_call(
        kernel,
        name=name,
        out_shape=outs,
        scratch_shapes=scratch,
        cost_estimate=pl.CostEstimate(flops=flops, bytes_accessed=work, transcendentals=0),
        compiler_params=pltpu.CompilerParams(vmem_limit_bytes=limit),
        **more,
    )


def shape(*dims):
    return jax.ShapeDtypeStruct(dims, bf16)


def layer_norm(values, gain, bias):
    average = jnp.mean(values, axis=0, keepdims=True)
    centred = values - average
    variance = jnp.mean(centred * centred, axis=0, keepdims=True)
    wide = values.shape[1] // 128
    return centred * lax.rsqrt(variance + epsilon) * jnp.tile(gain, (1, wide)) + jnp.tile(
        bias, (1, wide)
    )


def column(row):
    return jnp.broadcast_to(row, (128, 128)).T


def pair_order():
    def distance(pair):
        y, z = pair // 16, pair % 8
        return min(z, 8 - z)

    return [far_pair] + [pair for pair in sorted(range(64), key=distance) if pair != far_pair]


def peers(core):
    return [4 * pair + 2 * xl + core for pair in pair_order() for xl in range(2)]


def to_peers(rows):
    return jnp.concatenate([rows[8 * pair : 8 * pair + 8, :] for pair in pair_order()], axis=0)


def from_peers(rows):
    places = [pair_order().index(pair) for pair in range(64)]
    return jnp.concatenate([rows[8 * place : 8 * place + 8, :] for place in places], axis=0)


def position():
    return 2 * lax.axis_index("xl") + lax.axis_index("core")


def lay_out(*refs):
    sources, outs, shared, vectors = refs[:11], refs[11:15], refs[15], refs[16]
    field, weights, rows, semaphores = refs[17:]
    copies = [
        pltpu.make_async_copy(source, target, semaphores.at[at])
        for at, (source, target) in enumerate(
            zip(
                sources,
                [field]
                + [weights.at[w] for w in range(6)]
                + [vectors.at[pl.ds(v, 1)] for v in range(4)],
            )
        )
    ]
    for copy in copies:
        copy.start()
    for copy in copies:
        copy.wait()
    mine = position()
    for lane in range(4):
        rows[lane] = field[:, :, 128 * lane : 128 * (lane + 1)].astype(f32).reshape(256, 128)
    for step, out in enumerate(outs):
        for lane in range(4):
            at = slice(128 * lane, 128 * (lane + 1))
            for ii in range(2):
                out[32 * ii : 32 * (ii + 1), at] = rows[
                    lane, pl.ds(2 * (mine ^ step) + ii, 32, stride=8), :
                ].astype(bf16)
    for out, first in ((outs[0], 64), (outs[1], 64), (outs[2], 64), (shared, 0)):
        for lane in range(4):
            at = slice(128 * lane, 128 * (lane + 1))
            out[first : first + 32, at] = weights[lane]
            out[first + 32 : first + 48, at] = weights[
                4 + lane % 2, 16 * (lane // 2) : 16 * (lane // 2 + 1), :
            ]


def factors(in0, in1, in2, in3, shared3, vectors, out, normed_out, late, field, weights, rows):
    mine = position()
    for step, block in enumerate((in0, in1, in2, in3)):
        first = pl.multiple_of((mine ^ step) * 32, 32)
        for ii in range(2):
            field[ii, pl.ds(first, 32), :] = block[32 * ii : 32 * (ii + 1), :].astype(f32)
        block = (in0.at[64:112], in1.at[64:112], in2.at[64:112], shared3)[step]
        weights[pl.ds(first, 32), :] = block[0:32, :]
        late[pl.ds(first, 16), :] = block[32:48, 0:256]
        late[pl.ds(pl.multiple_of(first + 16, 16), 16), :] = block[32:48, 256:512]
    gains, biases = column(vectors[0:1]), column(vectors[1:2])
    for ii in range(2):
        normed = layer_norm(field[ii], gains, biases).astype(bf16)
        normed_out[ii] = normed

        def project(which):
            return jnp.dot(
                weights[:, 128 * which : 128 * (which + 1)], normed, preferred_element_type=f32
            )

        for side in range(2):
            factor = jax.nn.sigmoid(project(2 * side + 1)) * project(2 * side)
            for lane in range(4):
                rows[pl.ds(8 * side + 4 * ii + lane, 128, stride=16), :] = factor[
                    :, 128 * lane : 128 * (lane + 1)
                ]
    out[...] = rows[...].reshape(128, 16, 128).astype(bf16)


def gates(normed, late, kept, given, rows):
    core = lax.axis_index("core")
    for ii in range(2):
        value = jax.nn.sigmoid(jnp.dot(late[:, 0:128], normed[ii], preferred_element_type=f32))
        rows[...] = value.T
        rows[...] = to_peers(rows)
        for jj in range(2):
            kept[2 * ii + jj] = rows[pl.ds(2 * core + jj, 128, stride=4), :].astype(bf16)
            given[2 * ii + jj] = rows[pl.ds(2 * (1 - core) + jj, 128, stride=4), :].astype(bf16)


def prepare(own, left, right, received):
    core = lax.axis_index("core")
    received[...] = own[...].astype(f32).reshape(2048, 128)
    for lane in range(4):
        for ii in range(2):
            left[lane, pl.ds(2 * core + ii, 128, stride=4), :] = received[
                pl.ds(4 * ii + lane, 128, stride=16), :
            ]
            right[128 * ii : 128 * (ii + 1), 128 * lane : 128 * (lane + 1)] = received[
                pl.ds(8 + 4 * ii + lane, 128, stride=16), :
            ].astype(bf16)


def products(own_left, right, other, kept, given, out, received, left, rows):
    core = lax.axis_index("core")
    mine = lax.broadcasted_iota(jnp.int32, (512, 128), 0) // 2 % 2 == core
    received[...] = other[...].astype(f32).reshape(1024, 128)
    whole = []
    for lane in range(4):
        for ii in range(2):
            left[pl.ds(2 * (1 - core) + ii, 128, stride=4), :] = received[
                pl.ds(4 * ii + lane, 128, stride=8), :
            ]
        left[...] = jnp.where(mine, own_left[lane], left[...])
        whole.append(from_peers(left).astype(bf16))
    total = lax.dot_general(
        right[...],
        jnp.concatenate(whole, axis=1),
        (((1,), (1,)), ((), ())),
        preferred_element_type=f32,
    )
    for jj in range(2):
        for lane in range(4):
            rows[pl.ds(4 * jj + lane, 128, stride=16), :] = total[
                128 * jj : 128 * (jj + 1), 128 * lane : 128 * (lane + 1)
            ]
        for ii in range(2):
            at = 8 + 4 * jj + ii
            rows[pl.ds(at + 2 * core, 128, stride=16), :] = kept[2 * ii + jj].astype(f32)
            rows[pl.ds(at + 2 * (1 - core), 128, stride=16), :] = given[2 * ii + jj].astype(f32)
    out[...] = rows[...].reshape(128, 16, 128).astype(bf16)


def updates(got, late, vectors, out0, out1, out2, out3, rows, gate_rows, update):
    mine = position()
    rows[...] = got[...].astype(f32).reshape(2048, 128)
    gains, biases = column(vectors[2:3]), column(vectors[3:4])
    final = late[:, 128:256]
    for jj in range(2):
        for ii in range(4):
            gate_rows[pl.ds(ii, 128, stride=4), :] = rows[
                pl.ds(8 + 4 * jj + ii, 128, stride=16), :
            ]
        gating = from_peers(gate_rows).T
        for lane in range(4):
            hidden = rows[pl.ds(4 * jj + lane, 128, stride=16), :]
            normed = layer_norm(hidden, gains, biases).astype(bf16)
            value = jnp.dot(final, normed, preferred_element_type=f32)
            at = slice(128 * lane, 128 * (lane + 1))
            update[jj, :, at] = (value * gating[:, at]).astype(bf16)
    for step, out in enumerate((out0, out1, out2, out3)):
        out[...] = update[:, pl.ds(pl.multiple_of((mine ^ step) * 32, 32), 32), :]


def arrange(in0, in1, in2, in3, out, rows):
    mine = position()
    for lane in range(4):
        at = slice(128 * lane, 128 * (lane + 1))
        for step, block in enumerate((in0, in1, in2, in3)):
            for jj in range(2):
                rows[lane, pl.ds(2 * (mine ^ step) + jj, 32, stride=8), :] = block[
                    jj, :, at
                ].astype(f32)
        out[:, :, at] = rows[lane].reshape(32, 8, 128).astype(bf16)


def swap(array, step):
    return lax.ppermute(array, ("xl", "core"), [(s, s ^ step) for s in range(4)])


def around(array, step):
    pairs = [(s, s ^ (4 + step)) for s in range(8)]
    return lax.ppermute(array, ("xh", "xl", "core"), pairs)


def scatter(messages):
    return lax.all_to_all(
        messages,
        ("y", "xh", "z", "xl", "core"),
        0,
        0,
        axis_index_groups=[peers(0), peers(1)],
        tiled=True,
    )


def exchange(parts):
    return [parts[0]] + [swap(parts[step], step) for step in (1, 2, 3)]


def body(
    pair_field,
    input_gain,
    input_bias,
    left_weight,
    left_gate,
    right_weight,
    right_gate,
    gate_weight,
    output_gain,
    output_bias,
    final_weight,
):
    weights = (left_weight, left_gate, right_weight, right_gate, gate_weight, final_weight)
    vectors = (input_gain, input_bias, output_gain, output_bias)
    *parts, shared, vectors = call(
        lay_out,
        "lay_out",
        tuple(pltpu.VMEM((high, 512), bf16) for high in (112, 112, 112, 64, 48))
        + (pltpu.VMEM((4, 128), f32),),
        [
            pltpu.VMEM((32, 8, 512), bf16),
            pltpu.VMEM((6, 32, 128), bf16),
            pltpu.VMEM((4, 256, 128), f32),
            pltpu.SemaphoreType.DMA((11,)),
        ],
        limit=60 * 1024 * 1024,
        in_specs=[pl.BlockSpec(memory_space=pltpu.HBM)] * 11,
    )(pair_field, *[w.T for w in weights], *[v.reshape(1, 128) for v in vectors])
    sent, normed, late = call(
        factors,
        "factors",
        (shape(128, 16, 128), shape(2, 128, 512), shape(128, 256)),
        [
            pltpu.VMEM((2, 128, 512), f32),
            pltpu.VMEM((128, 512), bf16),
            pltpu.VMEM((2048, 128), f32),
        ],
    )(*exchange(parts), around(shared, 3), vectors)
    own = scatter(sent)
    kept, given = call(
        gates,
        "gates",
        (shape(4, 128, 128),) * 2,
        [pltpu.VMEM((512, 128), f32)],
        flops=1 << 30,
    )(normed, late)
    left, right = call(
        prepare,
        "prepare",
        (jax.ShapeDtypeStruct((4, 512, 128), f32), shape(256, 512)),
        [pltpu.VMEM((2048, 128), f32)],
        flops=1 << 30,
    )(own)
    sent = call(
        products,
        "products",
        shape(128, 16, 128),
        [
            pltpu.VMEM((1024, 128), f32),
            pltpu.VMEM((512, 128), f32),
            pltpu.VMEM((2048, 128), f32),
        ],
    )(left, right, swap(own[:, :8], 1), kept, swap(given, 1))
    got = scatter(sent)
    parts = call(
        updates,
        "updates",
        (shape(2, 32, 512),) * 4,
        [
            pltpu.VMEM((2048, 128), f32),
            pltpu.VMEM((512, 128), f32),
            pltpu.VMEM((2, 128, 512), bf16),
        ],
    )(got, late, vectors)
    return call(arrange, "arrange", shape(32, 8, 512), [pltpu.VMEM((4, 256, 128), f32)])(
        *exchange(parts)
    )


def solution(mesh):
    mesh = Mesh(mesh.devices.reshape(4, 2, 8, 2, 2), ("y", "xh", "z", "xl", "core"))
    row, ch = ("y", "xh", "z"), ("xl", "core")
    placed = (
        P(ch, row, None),
        P(),
        P(),
        P(None, ch),
        P(None, ch),
        P(None, ch),
        P(None, ch),
        P(None, ch),
        P(),
        P(),
        P(None, ch),
    )
    return jax.shard_map(
        body, mesh=mesh, in_specs=placed, out_specs=P(ch, row, None), check_vma=False
    )
```

```python
import jax
import jax.numpy as jnp
from jax import lax
from jax.experimental import pallas as pl
from jax.experimental.pallas import tpu as pltpu
from jax.sharding import Mesh
from jax.sharding import PartitionSpec as P

epsilon = 1e-05
far_pair = 45
bf16, f32 = jnp.bfloat16, jnp.float32
vmem_bytes = 16 * 1024 * 1024


def call(kernel, name, outs, scratch, flops=0, work=1 << 20, limit=vmem_bytes, **more):
    return pl.pallas_call(
        kernel,
        name=name,
        out_shape=outs,
        scratch_shapes=scratch,
        cost_estimate=pl.CostEstimate(flops=flops, bytes_accessed=work, transcendentals=0),
        compiler_params=pltpu.CompilerParams(vmem_limit_bytes=limit),
        **more,
    )


def shape(*dims):
    return jax.ShapeDtypeStruct(dims, bf16)


def layer_norm(values, gain, bias):
    average = jnp.mean(values, axis=0, keepdims=True)
    centred = values - average
    variance = jnp.mean(centred * centred, axis=0, keepdims=True)
    wide = values.shape[1] // 128
    return centred * lax.rsqrt(variance + epsilon) * jnp.tile(gain, (1, wide)) + jnp.tile(
        bias, (1, wide)
    )


def column(row):
    return jnp.broadcast_to(row, (128, 128)).T


def pair_order():
    def distance(pair):
        y, z = pair // 16, pair % 8
        return min(z, 8 - z)

    return [far_pair] + [pair for pair in sorted(range(64), key=distance) if pair != far_pair]


def peers(core):
    return [4 * pair + 2 * xl + core for pair in pair_order() for xl in range(2)]


def to_peers(rows):
    return jnp.concatenate([rows[8 * pair : 8 * pair + 8, :] for pair in pair_order()], axis=0)


def from_peers(rows):
    places = [pair_order().index(pair) for pair in range(64)]
    return jnp.concatenate([rows[8 * place : 8 * place + 8, :] for place in places], axis=0)


def position():
    return 2 * lax.axis_index("xl") + lax.axis_index("core")


def lay_out(*refs):
    sources, outs, shared, vectors = refs[:11], refs[11:15], refs[15], refs[16]
    field, weights, rows, semaphores = refs[17:]
    copies = [
        pltpu.make_async_copy(source, target, semaphores.at[at])
        for at, (source, target) in enumerate(
            zip(
                sources,
                [field]
                + [weights.at[w] for w in range(6)]
                + [vectors.at[pl.ds(v, 1)] for v in range(4)],
            )
        )
    ]
    for copy in copies:
        copy.start()
    for copy in copies:
        copy.wait()
    mine = position()
    for lane in range(4):
        rows[lane] = field[:, :, 128 * lane : 128 * (lane + 1)].astype(f32).reshape(256, 128)
    for step, out in enumerate(outs):
        for lane in range(4):
            at = slice(128 * lane, 128 * (lane + 1))
            for ii in range(2):
                out[32 * ii : 32 * (ii + 1), at] = rows[
                    lane, pl.ds(2 * (mine ^ step) + ii, 32, stride=8), :
                ].astype(bf16)
    for out, first in ((outs[0], 64), (outs[1], 64), (outs[2], 64), (shared, 0)):
        for lane in range(4):
            at = slice(128 * lane, 128 * (lane + 1))
            out[first : first + 32, at] = weights[lane]
            out[first + 32 : first + 48, at] = weights[
                4 + lane % 2, 16 * (lane // 2) : 16 * (lane // 2 + 1), :
            ]


def factors(in0, in1, in2, in3, shared3, vectors, out, normed_out, late, field, weights, rows):
    mine = position()
    for step, block in enumerate((in0, in1, in2, in3)):
        first = pl.multiple_of((mine ^ step) * 32, 32)
        for ii in range(2):
            field[ii, pl.ds(first, 32), :] = block[32 * ii : 32 * (ii + 1), :].astype(f32)
        block = (in0.at[64:112], in1.at[64:112], in2.at[64:112], shared3)[step]
        weights[pl.ds(first, 32), :] = block[0:32, :]
        late[pl.ds(first, 16), :] = block[32:48, 0:256]
        late[pl.ds(pl.multiple_of(first + 16, 16), 16), :] = block[32:48, 256:512]
    gains, biases = column(vectors[0:1]), column(vectors[1:2])
    for ii in range(2):
        normed = layer_norm(field[ii], gains, biases).astype(bf16)
        normed_out[ii] = normed

        def project(which):
            return jnp.dot(
                weights[:, 128 * which : 128 * (which + 1)], normed, preferred_element_type=f32
            )

        for side in range(2):
            factor = jax.nn.sigmoid(project(2 * side + 1)) * project(2 * side)
            for lane in range(4):
                rows[pl.ds(8 * side + 4 * ii + lane, 128, stride=16), :] = factor[
                    :, 128 * lane : 128 * (lane + 1)
                ]
    out[...] = rows[...].reshape(128, 16, 128).astype(bf16)


def gates(normed, late, kept, given, rows):
    core = lax.axis_index("core")
    for ii in range(2):
        value = jax.nn.sigmoid(jnp.dot(late[:, 0:128], normed[ii], preferred_element_type=f32))
        rows[...] = value.T
        rows[...] = to_peers(rows)
        for jj in range(2):
            kept[2 * ii + jj] = rows[pl.ds(2 * core + jj, 128, stride=4), :].astype(bf16)
            given[2 * ii + jj] = rows[pl.ds(2 * (1 - core) + jj, 128, stride=4), :].astype(bf16)


def prepare(own, left, right, received):
    core = lax.axis_index("core")
    received[...] = own[...].astype(f32).reshape(2048, 128)
    for lane in range(4):
        for ii in range(2):
            left[lane, pl.ds(2 * core + ii, 128, stride=4), :] = received[
                pl.ds(4 * ii + lane, 128, stride=16), :
            ]
            right[128 * ii : 128 * (ii + 1), 128 * lane : 128 * (lane + 1)] = received[
                pl.ds(8 + 4 * ii + lane, 128, stride=16), :
            ].astype(bf16)


def products(own_left, right, other, kept, given, out, received, left, rows):
    core = lax.axis_index("core")
    mine = lax.broadcasted_iota(jnp.int32, (512, 128), 0) // 2 % 2 == core
    received[...] = other[...].astype(f32).reshape(1024, 128)
    whole = []
    for lane in range(4):
        for ii in range(2):
            left[pl.ds(2 * (1 - core) + ii, 128, stride=4), :] = received[
                pl.ds(4 * ii + lane, 128, stride=8), :
            ]
        left[...] = jnp.where(mine, own_left[lane], left[...])
        whole.append(from_peers(left).astype(bf16))
    total = lax.dot_general(
        right[...],
        jnp.concatenate(whole, axis=1),
        (((1,), (1,)), ((), ())),
        preferred_element_type=f32,
    )
    for jj in range(2):
        for lane in range(4):
            rows[pl.ds(4 * jj + lane, 128, stride=16), :] = total[
                128 * jj : 128 * (jj + 1), 128 * lane : 128 * (lane + 1)
            ]
        for ii in range(2):
            at = 8 + 4 * jj + ii
            rows[pl.ds(at + 2 * core, 128, stride=16), :] = kept[2 * ii + jj].astype(f32)
            rows[pl.ds(at + 2 * (1 - core), 128, stride=16), :] = given[2 * ii + jj].astype(f32)
    out[...] = rows[...].reshape(128, 16, 128).astype(bf16)


def finish(late, normed, gating, *outs):
    for out, step in outs:
        some = pl.ds(pl.multiple_of((position() ^ step) * 32, 32), 32)
        final = late[some, 128:256]
        for jj in range(2):
            value = jnp.dot(final, normed[jj], preferred_element_type=f32)
            out[jj] = (value * gating[jj, some, :].astype(f32)).astype(bf16)


def updates(got, late, vectors, out1, out2, out3, normed, gating, rows, gate_rows):
    rows[...] = got[...].astype(f32).reshape(2048, 128)
    gains, biases = column(vectors[2:3]), column(vectors[3:4])
    for jj in range(2):
        for ii in range(4):
            gate_rows[pl.ds(ii, 128, stride=4), :] = rows[
                pl.ds(8 + 4 * jj + ii, 128, stride=16), :
            ]
        gating[jj] = from_peers(gate_rows).T.astype(bf16)
        for lane in range(4):
            hidden = rows[pl.ds(4 * jj + lane, 128, stride=16), :]
            at = slice(128 * lane, 128 * (lane + 1))
            normed[jj, :, at] = layer_norm(hidden, gains, biases).astype(bf16)
    finish(late, normed, gating, (out1, 1), (out2, 2), (out3, 3))


def updates_near(late, normed, gating, out0):
    finish(late, normed, gating, (out0, 0))


def arrange(in0, in1, in2, in3, out, rows):
    mine = position()
    for lane in range(4):
        at = slice(128 * lane, 128 * (lane + 1))
        for step, block in enumerate((in0, in1, in2, in3)):
            for jj in range(2):
                rows[lane, pl.ds(2 * (mine ^ step) + jj, 32, stride=8), :] = block[
                    jj, :, at
                ].astype(f32)
        out[:, :, at] = rows[lane].reshape(32, 8, 128).astype(bf16)


def swap(array, step):
    return lax.ppermute(array, ("xl", "core"), [(s, s ^ step) for s in range(4)])


def around(array, step):
    pairs = [(s, s ^ (4 + step)) for s in range(8)]
    return lax.ppermute(array, ("xh", "xl", "core"), pairs)


def scatter(messages):
    return lax.all_to_all(
        messages,
        ("y", "xh", "z", "xl", "core"),
        0,
        0,
        axis_index_groups=[peers(0), peers(1)],
        tiled=True,
    )


def exchange(parts, *steps):
    return [parts[0]] + [swap(parts[step], step) for step in steps]


def body(
    pair_field,
    input_gain,
    input_bias,
    left_weight,
    left_gate,
    right_weight,
    right_gate,
    gate_weight,
    output_gain,
    output_bias,
    final_weight,
):
    weights = (left_weight, left_gate, right_weight, right_gate, gate_weight, final_weight)
    vectors = (input_gain, input_bias, output_gain, output_bias)
    *parts, shared, vectors = call(
        lay_out,
        "lay_out",
        tuple(pltpu.VMEM((high, 512), bf16) for high in (112, 112, 112, 64, 48))
        + (pltpu.VMEM((4, 128), f32),),
        [
            pltpu.VMEM((32, 8, 512), bf16),
            pltpu.VMEM((6, 32, 128), bf16),
            pltpu.VMEM((4, 256, 128), f32),
            pltpu.SemaphoreType.DMA((11,)),
        ],
        limit=60 * 1024 * 1024,
        in_specs=[pl.BlockSpec(memory_space=pltpu.HBM)] * 11,
    )(pair_field, *[w.T for w in weights], *[v.reshape(1, 128) for v in vectors])
    sent, normed, late = call(
        factors,
        "factors",
        (shape(128, 16, 128), shape(2, 128, 512), shape(128, 256)),
        [
            pltpu.VMEM((2, 128, 512), f32),
            pltpu.VMEM((128, 512), bf16),
            pltpu.VMEM((2048, 128), f32),
        ],
    )(*exchange(parts, 1, 2, 3), around(shared, 3), vectors)
    own = scatter(sent)
    kept, given = call(
        gates,
        "gates",
        (shape(4, 128, 128),) * 2,
        [pltpu.VMEM((512, 128), f32)],
        flops=1 << 30,
    )(normed, late)
    left, right = call(
        prepare,
        "prepare",
        (jax.ShapeDtypeStruct((4, 512, 128), f32), shape(256, 512)),
        [pltpu.VMEM((2048, 128), f32)],
        flops=1 << 30,
    )(own)
    sent = call(
        products,
        "products",
        shape(128, 16, 128),
        [
            pltpu.VMEM((1024, 128), f32),
            pltpu.VMEM((512, 128), f32),
            pltpu.VMEM((2048, 128), f32),
        ],
    )(left, right, swap(own[:, :8], 1), kept, swap(given, 1))
    got = scatter(sent)
    out1, out2, out3, normed, gating = call(
        updates,
        "updates",
        (shape(2, 32, 512),) * 3 + (shape(2, 128, 512),) * 2,
        [pltpu.VMEM((2048, 128), f32), pltpu.VMEM((512, 128), f32)],
    )(got, late, vectors)
    near = call(updates_near, "updates_near", shape(2, 32, 512), [], flops=1 << 30)(
        late, normed, gating
    )
    parts = (near, out1, out2, out3)
    return call(arrange, "arrange", shape(32, 8, 512), [pltpu.VMEM((4, 256, 128), f32)])(
        *exchange(parts, 1, 2, 3)
    )


def solution(mesh):
    mesh = Mesh(mesh.devices.reshape(4, 2, 8, 2, 2), ("y", "xh", "z", "xl", "core"))
    row, ch = ("y", "xh", "z"), ("xl", "core")
    placed = (
        P(ch, row, None),
        P(),
        P(),
        P(None, ch),
        P(None, ch),
        P(None, ch),
        P(None, ch),
        P(None, ch),
        P(),
        P(),
        P(None, ch),
    )
    return jax.shard_map(
        body, mesh=mesh, in_specs=placed, out_specs=P(ch, row, None), check_vma=False
    )
```

```python
import jax
import jax.numpy as jnp
from jax import lax
from jax.experimental import pallas as pl
from jax.experimental.pallas import tpu as pltpu
from jax.sharding import Mesh
from jax.sharding import PartitionSpec as P

epsilon = 1e-05
far_pair = 45
bf16, f32 = jnp.bfloat16, jnp.float32
vmem_bytes = 16 * 1024 * 1024


def call(kernel, name, outs, scratch, flops=0, work=1 << 20, limit=vmem_bytes, **more):
    return pl.pallas_call(
        kernel,
        name=name,
        out_shape=outs,
        scratch_shapes=scratch,
        cost_estimate=pl.CostEstimate(flops=flops, bytes_accessed=work, transcendentals=0),
        compiler_params=pltpu.CompilerParams(vmem_limit_bytes=limit),
        **more,
    )


def shape(*dims):
    return jax.ShapeDtypeStruct(dims, bf16)


def layer_norm(values, gain, bias):
    average = jnp.mean(values, axis=0, keepdims=True)
    centred = values - average
    variance = jnp.mean(centred * centred, axis=0, keepdims=True)
    wide = values.shape[1] // 128
    return centred * lax.rsqrt(variance + epsilon) * jnp.tile(gain, (1, wide)) + jnp.tile(
        bias, (1, wide)
    )


def column(row):
    return jnp.broadcast_to(row, (128, 128)).T


def pair_order():
    def distance(pair):
        y, z = pair // 16, pair % 8
        return min(z, 8 - z)

    return [far_pair] + [pair for pair in sorted(range(64), key=distance) if pair != far_pair]


def peers(core):
    return [4 * pair + 2 * xl + core for pair in pair_order() for xl in range(2)]


def to_peers(rows):
    return jnp.concatenate([rows[8 * pair : 8 * pair + 8, :] for pair in pair_order()], axis=0)


def from_peers(rows):
    places = [pair_order().index(pair) for pair in range(64)]
    return jnp.concatenate([rows[8 * place : 8 * place + 8, :] for place in places], axis=0)


def position():
    return 2 * lax.axis_index("xl") + lax.axis_index("core")


def lay_out(*refs):
    sources, outs, shared, vectors = refs[:11], refs[11:15], refs[15], refs[16]
    field, weights, rows, semaphores = refs[17:]
    copies = [
        pltpu.make_async_copy(source, target, semaphores.at[at])
        for at, (source, target) in enumerate(
            zip(
                sources,
                [field]
                + [weights.at[w] for w in range(6)]
                + [vectors.at[pl.ds(v, 1)] for v in range(4)],
            )
        )
    ]
    for copy in copies:
        copy.start()
    for copy in copies:
        copy.wait()
    mine = position()
    for lane in range(4):
        rows[lane] = field[:, :, 128 * lane : 128 * (lane + 1)].astype(f32).reshape(256, 128)
    for step, out in enumerate(outs):
        for lane in range(4):
            at = slice(128 * lane, 128 * (lane + 1))
            for ii in range(2):
                out[32 * ii : 32 * (ii + 1), at] = rows[
                    lane, pl.ds(2 * (mine ^ step) + ii, 32, stride=8), :
                ].astype(bf16)
    for out, first in ((outs[0], 64), (outs[1], 64), (outs[2], 64), (shared, 0)):
        for lane in range(4):
            at = slice(128 * lane, 128 * (lane + 1))
            out[first : first + 32, at] = weights[lane]
            out[first + 32 : first + 48, at] = weights[
                4 + lane % 2, 16 * (lane // 2) : 16 * (lane // 2 + 1), :
            ]


def factors(in0, in1, in2, in3, shared3, vectors, out, normed_out, late, field, weights, rows):
    mine = position()
    for step, block in enumerate((in0, in1, in2, in3)):
        first = pl.multiple_of((mine ^ step) * 32, 32)
        for ii in range(2):
            field[ii, pl.ds(first, 32), :] = block[32 * ii : 32 * (ii + 1), :].astype(f32)
        block = (in0.at[64:112], in1.at[64:112], in2.at[64:112], shared3)[step]
        weights[pl.ds(first, 32), :] = block[0:32, :]
        late[pl.ds(first, 16), :] = block[32:48, 0:256]
        late[pl.ds(pl.multiple_of(first + 16, 16), 16), :] = block[32:48, 256:512]
    gains, biases = column(vectors[0:1]), column(vectors[1:2])
    for ii in range(2):
        normed = layer_norm(field[ii], gains, biases).astype(bf16)
        normed_out[ii] = normed

        def project(which):
            return jnp.dot(
                weights[:, 128 * which : 128 * (which + 1)], normed, preferred_element_type=f32
            )

        for side in range(2):
            gate = 0.5 * jnp.tanh(0.5 * project(2 * side + 1)) + 0.5
            factor = gate * project(2 * side)
            for lane in range(4):
                rows[pl.ds(8 * side + 4 * ii + lane, 128, stride=16), :] = factor[
                    :, 128 * lane : 128 * (lane + 1)
                ]
    out[...] = rows[...].reshape(128, 16, 128).astype(bf16)


def gates(normed, late, kept, given, rows):
    core = lax.axis_index("core")
    for ii in range(2):
        value = jax.nn.sigmoid(jnp.dot(late[:, 0:128], normed[ii], preferred_element_type=f32))
        rows[...] = value.T
        rows[...] = to_peers(rows)
        for jj in range(2):
            kept[2 * ii + jj] = rows[pl.ds(2 * core + jj, 128, stride=4), :].astype(bf16)
            given[2 * ii + jj] = rows[pl.ds(2 * (1 - core) + jj, 128, stride=4), :].astype(bf16)


def prepare(own, left, right, received):
    core = lax.axis_index("core")
    received[...] = own[...].astype(f32).reshape(2048, 128)
    for lane in range(4):
        for ii in range(2):
            left[lane, pl.ds(2 * core + ii, 128, stride=4), :] = received[
                pl.ds(4 * ii + lane, 128, stride=16), :
            ]
            right[128 * ii : 128 * (ii + 1), 128 * lane : 128 * (lane + 1)] = received[
                pl.ds(8 + 4 * ii + lane, 128, stride=16), :
            ].astype(bf16)


def products(own_left, right, other, kept, given, out, received, left, rows):
    core = lax.axis_index("core")
    mine = lax.broadcasted_iota(jnp.int32, (512, 128), 0) // 2 % 2 == core
    received[...] = other[...].astype(f32).reshape(1024, 128)
    whole = []
    for lane in range(4):
        for ii in range(2):
            left[pl.ds(2 * (1 - core) + ii, 128, stride=4), :] = received[
                pl.ds(4 * ii + lane, 128, stride=8), :
            ]
        left[...] = jnp.where(mine, own_left[lane], left[...])
        whole.append(from_peers(left).astype(bf16))
    total = lax.dot_general(
        right[...],
        jnp.concatenate(whole, axis=1),
        (((1,), (1,)), ((), ())),
        preferred_element_type=f32,
    )
    for jj in range(2):
        for lane in range(4):
            rows[pl.ds(4 * jj + lane, 128, stride=16), :] = total[
                128 * jj : 128 * (jj + 1), 128 * lane : 128 * (lane + 1)
            ]
        for ii in range(2):
            at = 8 + 4 * jj + ii
            rows[pl.ds(at + 2 * core, 128, stride=16), :] = kept[2 * ii + jj].astype(f32)
            rows[pl.ds(at + 2 * (1 - core), 128, stride=16), :] = given[2 * ii + jj].astype(f32)
    out[...] = rows[...].reshape(128, 16, 128).astype(bf16)


def finish(late, normed, gating, *outs):
    for out, step in outs:
        some = pl.ds(pl.multiple_of((position() ^ step) * 32, 32), 32)
        final = late[some, 128:256]
        for jj in range(2):
            value = jnp.dot(final, normed[jj], preferred_element_type=f32)
            out[jj] = (value * gating[jj, some, :].astype(f32)).astype(bf16)


def updates(got, late, vectors, out1, out2, out3, normed, gating, rows, gate_rows):
    rows[...] = got[...].astype(f32).reshape(2048, 128)
    gains, biases = column(vectors[2:3]), column(vectors[3:4])
    for jj in range(2):
        for ii in range(4):
            gate_rows[pl.ds(ii, 128, stride=4), :] = rows[
                pl.ds(8 + 4 * jj + ii, 128, stride=16), :
            ]
        gating[jj] = from_peers(gate_rows).T.astype(bf16)
        for lane in range(4):
            hidden = rows[pl.ds(4 * jj + lane, 128, stride=16), :]
            at = slice(128 * lane, 128 * (lane + 1))
            normed[jj, :, at] = layer_norm(hidden, gains, biases).astype(bf16)
    finish(late, normed, gating, (out1, 1), (out2, 2), (out3, 3))


def updates_near(late, normed, gating, out0):
    finish(late, normed, gating, (out0, 0))


def arrange(in0, in1, in2, in3, out, rows):
    mine = position()
    for lane in range(4):
        at = slice(128 * lane, 128 * (lane + 1))
        for step, block in enumerate((in0, in1, in2, in3)):
            for jj in range(2):
                rows[lane, pl.ds(2 * (mine ^ step) + jj, 32, stride=8), :] = block[
                    jj, :, at
                ].astype(f32)
        out[:, :, at] = rows[lane].reshape(32, 8, 128).astype(bf16)


def swap(array, step):
    return lax.ppermute(array, ("xl", "core"), [(s, s ^ step) for s in range(4)])


def around(array, step):
    pairs = [(s, s ^ (4 + step)) for s in range(8)]
    return lax.ppermute(array, ("xh", "xl", "core"), pairs)


def scatter(messages):
    return lax.all_to_all(
        messages,
        ("y", "xh", "z", "xl", "core"),
        0,
        0,
        axis_index_groups=[peers(0), peers(1)],
        tiled=True,
    )


def exchange(parts, *steps):
    return [parts[0]] + [swap(parts[step], step) for step in steps]


def body(
    pair_field,
    input_gain,
    input_bias,
    left_weight,
    left_gate,
    right_weight,
    right_gate,
    gate_weight,
    output_gain,
    output_bias,
    final_weight,
):
    weights = (left_weight, left_gate, right_weight, right_gate, gate_weight, final_weight)
    vectors = (input_gain, input_bias, output_gain, output_bias)
    *parts, shared, vectors = call(
        lay_out,
        "lay_out",
        tuple(pltpu.VMEM((high, 512), bf16) for high in (112, 112, 112, 64, 48))
        + (pltpu.VMEM((4, 128), f32),),
        [
            pltpu.VMEM((32, 8, 512), bf16),
            pltpu.VMEM((6, 32, 128), bf16),
            pltpu.VMEM((4, 256, 128), f32),
            pltpu.SemaphoreType.DMA((11,)),
        ],
        limit=60 * 1024 * 1024,
        in_specs=[pl.BlockSpec(memory_space=pltpu.HBM)] * 11,
    )(pair_field, *[w.T for w in weights], *[v.reshape(1, 128) for v in vectors])
    sent, normed, late = call(
        factors,
        "factors",
        (shape(128, 16, 128), shape(2, 128, 512), shape(128, 256)),
        [
            pltpu.VMEM((2, 128, 512), f32),
            pltpu.VMEM((128, 512), bf16),
            pltpu.VMEM((2048, 128), f32),
        ],
    )(*exchange(parts, 1, 2, 3), around(shared, 3), vectors)
    own = scatter(sent)
    kept, given = call(
        gates,
        "gates",
        (shape(4, 128, 128),) * 2,
        [pltpu.VMEM((512, 128), f32)],
        flops=1 << 30,
    )(normed, late)
    left, right = call(
        prepare,
        "prepare",
        (jax.ShapeDtypeStruct((4, 512, 128), f32), shape(256, 512)),
        [pltpu.VMEM((2048, 128), f32)],
        flops=1 << 30,
    )(own)
    sent = call(
        products,
        "products",
        shape(128, 16, 128),
        [
            pltpu.VMEM((1024, 128), f32),
            pltpu.VMEM((512, 128), f32),
            pltpu.VMEM((2048, 128), f32),
        ],
    )(left, right, swap(own[:, :8], 1), kept, swap(given, 1))
    got = scatter(sent)
    out1, out2, out3, normed, gating = call(
        updates,
        "updates",
        (shape(2, 32, 512),) * 3 + (shape(2, 128, 512),) * 2,
        [pltpu.VMEM((2048, 128), f32), pltpu.VMEM((512, 128), f32)],
    )(got, late, vectors)
    near = call(updates_near, "updates_near", shape(2, 32, 512), [], flops=1 << 30)(
        late, normed, gating
    )
    parts = (near, out1, out2, out3)
    return call(arrange, "arrange", shape(32, 8, 512), [pltpu.VMEM((4, 256, 128), f32)])(
        *exchange(parts, 1, 2, 3)
    )


def solution(mesh):
    mesh = Mesh(mesh.devices.reshape(4, 2, 8, 2, 2), ("y", "xh", "z", "xl", "core"))
    row, ch = ("y", "xh", "z"), ("xl", "core")
    placed = (
        P(ch, row, None),
        P(),
        P(),
        P(None, ch),
        P(None, ch),
        P(None, ch),
        P(None, ch),
        P(None, ch),
        P(),
        P(),
        P(None, ch),
    )
    return jax.shard_map(
        body, mesh=mesh, in_specs=placed, out_specs=P(ch, row, None), check_vma=False
    )
```
